256 devices in a mesh: dom: 64 (over x, z, core), mp: 4 (over y).
Axes of the slice: x: 4, y: 4, z: 8, core: 2. Of those that a mesh axis runs over, the one named last changes fastest.
Arguments:
- hidden_states: bfloat16 [32768, 768], P('dom'), may hold values from -6.5 to 6.5
- text_len: int32 [256], P('dom'), may hold values from 16 to 128
- w_qkv: bfloat16 [768, 3, 768], P(None, None, 'mp'), may hold values from -8 to 8
- w_out: bfloat16 [768, 768], P('mp'), may hold values from -0.21875 to 0.21875
- w_up: bfloat16 [768, 3072], P(None, 'mp'), may hold values from -0.21875 to 0.21875
- w_down: bfloat16 [3072, 768], P('mp'), may hold values from -0.109375 to 0.109375
- hist: bfloat16 [16384, 768], P('dom'), may hold values from -16 to 16
- nbr: int32 [16384, 10], P('dom'), may hold values from 0 to 1279, as said below
- send_rows: int32 [64, 64, 16], P('dom'), may hold values from -1 to 255, as said below
- fresh_target: int32 [256], replicated, may hold values from 0 to 16383, as said below
- w_self: bfloat16 [768, 768], P(None, 'mp'), may hold values from -0.21875 to 0.21875
- w_neigh: bfloat16 [768, 768], P(None, 'mp'), may hold values from -0.21875 to 0.21875
- upstream: bfloat16 [16384, 768], P('dom', 'mp'), may hold values from -6 to 6
Outputs:
- sage_out: bfloat16 [16384, 768], P('dom', 'mp')
- grad_fresh: float32 [256, 768], P('dom', 'mp')
- grad_self_w: float32 [768, 768], P('dom', 'mp')
- grad_neigh_w: float32 [768, 768], P('dom', 'mp')
The draws below stay inside these ranges and needn't reach their ends.
Inputs may be any that keep to these rules, and one draw needn't show every extreme that they name: `send_rows`: within each list the filled slots come first and -1 marks the unused ones; no partition lists rows for itself; every partition sends one row or more to every other, and for every partition some list to another partition fills all 16 slots. `nbr`: an entry below 256 is a local row of the node's partition; an entry 256 + q * 16 + c reads slot c of the list partition q sends to the node's partition, always a filled slot of another partition's list. `fresh_target`: distinct rows; each partition owns exactly 4 of them.
All inputs are finite; a program needn't handle non-finite values.
Results may differ from the reference program's by a relative error of at most 0.015.
Values may be sent and summed in bfloat16 or wider, within the bound.
No kernel may reach another device: no remote copies, remote signals or barrier semaphores. Data moves between devices by JAX's collectives and lax.ppermute only.
A program may use at most 64 MiB of HBM per device.

```python
import math
import jax
import jax.numpy as jnp
from jax import lax

D = 768
HEADS = 12
FF = 3072
L = 128
K = 10
ENC_DEV = 4
G = 256
CAP = 16
NODES = 16384
ENC_TOTAL = 256
N_DOM = 64


def layout(key):
    peers = NODES // G
    key_count, key_full, key_fresh, key_order, key_offset, key_stride, key_place, key_pick = jax.random.split(key, 8)
    counts = jax.random.randint(key_count, (peers, peers), 1, CAP + 1)
    lift = jax.random.randint(key_full, (peers,), 1, peers)
    full_peer = (jnp.arange(peers) + lift) % peers
    counts = jnp.where(jnp.arange(peers)[None, :] == full_peer[:, None], CAP, counts)
    counts = jnp.where(jnp.eye(peers, dtype=bool), 0, counts)
    fresh_rows = jax.vmap(lambda sub_key: jax.random.permutation(sub_key, G)[:ENC_DEV])(jax.random.split(key_fresh, peers))
    order = jax.random.permutation(key_order, ENC_TOTAL)
    owner_part = order // ENC_DEV
    fresh_target = owner_part * G + fresh_rows[owner_part, order % ENC_DEV]
    offset = jax.random.randint(key_offset, (peers, peers, 1), 0, G)
    stride = 2 * jax.random.randint(key_stride, (peers, peers, 1), 0, max(G // 2, 1)) + 1
    slots = jnp.arange(CAP)[None, None, :]
    drawn = (offset + slots * stride) % G
    place = jax.random.randint(key_place, (peers, peers, 1), 0, jnp.maximum(counts, 1)[:, :, None])
    choose = jax.random.randint(key_pick, (peers, peers, 1), 0, ENC_DEV)
    fresh_here = fresh_rows[jnp.arange(peers)[:, None, None], choose]
    listed = jnp.where(slots == place, fresh_here, drawn)
    listed = jnp.where(slots < counts[:, :, None], listed, -1)
    return (counts, fresh_target.astype(jnp.int32), listed.astype(jnp.int32))


def draw_send_rows(key, part):
    return layout(key)[2]


def draw_fresh_target(key, part):
    return layout(key)[1]


def draw_nbr(key, part):
    counts = layout(key)[0]
    key = jax.random.fold_in(key, 11)
    key_remote, key_lift, key_slot, key_local = jax.random.split(key, 4)
    peers = NODES // G
    owner_part = (jnp.arange(NODES) // G)[:, None]
    remote = jax.random.randint(key_remote, (NODES, K), 0, 2)
    lift = jax.random.randint(key_lift, (NODES, K), 1, peers)
    source = (owner_part + lift) % peers
    limit = counts[source, owner_part]
    chosen_slot = jax.random.randint(key_slot, (NODES, K), 0, limit)
    local_row = jax.random.randint(key_local, (NODES, K), 0, G)
    return jnp.where(remote == 1, G + source * CAP + chosen_slot, local_row).astype(jnp.int32)


def draw_w_qkv(key, part):
    key = jax.random.fold_in(key, 5)
    key_base = jax.random.fold_in(key, 0)
    values = jnp.clip(jax.random.normal(key_base, (D, 3, D), jnp.float32), -6.0, 6.0) * D ** (-0.5)
    return values.astype(jnp.bfloat16)


def draw_hidden_states(key, part):
    key = jax.random.fold_in(key, 7)
    values = jnp.clip(jax.random.normal(key, (ENC_TOTAL * L, D), jnp.float32), -6.0, 6.0)
    return values.astype(jnp.bfloat16)


def place_ends(array, key, low, largest):
    spot = [jax.random.randint(jax.random.fold_in(key, axis), (), 0, length) for axis, length in enumerate(array.shape)]
    widest = array.shape.index(max(array.shape))
    beside = spot[:widest] + [(spot[widest] + 1) % array.shape[widest]] + spot[widest + 1:]
    return array.at[tuple(spot)].set(low).at[tuple(beside)].set(largest)


def with_spikes(array, own_key, source, target, shards_of, factor):
    owner, partner = [(jnp.arange(array.shape[axis_at]) // (array.shape[axis_at] // shards_of)).reshape([-1 if axis == axis_at else 1 for axis in range(array.ndim)]) for axis_at in (source, target)]
    chosen = jax.random.permutation(own_key, shards_of)[partner]
    strong = (owner == chosen) | (owner == (partner + shards_of // 2) % shards_of)
    return jnp.where(strong, factor * array, array)


def level_of(stream_key, extent, cuts, least, high):
    loudness = 1.0
    for axis_at, shards_of in cuts:
        heights = jax.random.uniform(jax.random.fold_in(jax.random.fold_in(stream_key, 6), axis_at), (shards_of,), jnp.float32, least / len(cuts), high / len(cuts))
        loudness = loudness * jnp.repeat(jnp.exp(heights), extent[axis_at] // shards_of).reshape((-1,) + (1,) * (len(extent) - 1 - axis_at))
    return loudness


def normal_values(key, extent, scale, most, shards=(), held_as=jnp.bfloat16):
    values = jax.random.normal(key, extent, jnp.float32) * scale
    if len(shards) > 0:
        values = level_of(key, extent, shards, -0.22, 0.18) * values
    return jnp.clip(values, min=-most, max=most).astype(held_as)


def heavy_noise(rng, dims, scale, most, cuts, heavy, kind=jnp.bfloat16):
    drawn = scale * jax.random.normal(rng, dims, jnp.float32)
    if cuts:
        drawn = drawn * level_of(rng, dims, cuts, -0.22, 0.18)
    return jnp.clip(with_spikes(drawn, jax.random.fold_in(rng, 3), *heavy), -most, most).astype(kind)


def setup_inputs(seed: int = 0) -> dict:
    streams_of = jax.random.split(jax.random.key(seed), 14)
    return {
        "hidden_states": draw_hidden_states(jax.random.fold_in(streams_of[13], 71), 0),
        "text_len": place_ends(jax.random.randint(streams_of[1], (ENC_TOTAL,), L // 8, L + 1), jax.random.fold_in(streams_of[1], 1), L // 8, L).astype(jnp.int32),
        "w_qkv": draw_w_qkv(jax.random.fold_in(streams_of[13], 71), 0),
        "w_out": normal_values(streams_of[3], (D, D), D ** -0.5, 0.21875, ((0, 4),)),
        "w_up": normal_values(streams_of[4], (D, FF), D ** -0.5, 0.21875, ((1, 4),)),
        "w_down": normal_values(streams_of[5], (FF, D), FF ** -0.5, 0.109375, ((0, 4),)),
        "hist": heavy_noise(streams_of[6], (NODES, D), 1.0, 16.0, ((0, 64),), (0, 1, 64, 4.0)),
        "nbr": draw_nbr(jax.random.fold_in(streams_of[13], 71), 0),
        "send_rows": draw_send_rows(jax.random.fold_in(streams_of[13], 71), 0),
        "fresh_target": draw_fresh_target(jax.random.fold_in(streams_of[13], 71), 0),
        "w_self": normal_values(streams_of[10], (D, D), D ** -0.5, 0.21875, ((1, 4),)),
        "w_neigh": normal_values(streams_of[11], (D, D), D ** -0.5, 0.21875, ((1, 4),)),
        "upstream": normal_values(streams_of[12], (NODES, D), 1.0, 6.0, ((0, 64), (1, 4))),
    }


EPSILON = 1e-05

def layer_norm(values):
    center = values - lax.optimization_barrier(jnp.mean(values, axis=-1, keepdims=True))
    spread = lax.optimization_barrier(jnp.mean(center * center, axis=-1, keepdims=True))
    return center * lax.rsqrt(spread + EPSILON)

def exact_gelu(values):
    return jax.nn.gelu(values, approximate=False)

def encode(hidden_states, text_len, w_qkv, w_out, w_up, w_down):
    text_count = text_len.shape[0]
    head_dim = D // HEADS
    packed = jnp.dot(hidden_states, w_qkv.reshape(D, 3 * D), preferred_element_type=jnp.float32).astype(jnp.bfloat16)
    packed = packed.reshape(text_count, L, 3, HEADS, head_dim)
    queries = packed[:, :, 0].astype(jnp.float32)
    keys_all = packed[:, :, 1].astype(jnp.float32)
    values_all = packed[:, :, 2].astype(jnp.float32)
    scores = jnp.einsum('tqhc,tkhc->thqk', queries, keys_all) / math.sqrt(head_dim)
    live_keys = jnp.arange(L, dtype=jnp.int32)[None, :] < text_len[:, None]
    scores = jnp.where(live_keys[:, None, None, :], scores, -1e+30)
    row_peak = lax.optimization_barrier(jnp.max(scores, axis=-1, keepdims=True))
    weights = jnp.exp(scores - row_peak)
    attention_probs = (weights / lax.optimization_barrier(jnp.sum(weights, axis=-1, keepdims=True))).astype(jnp.bfloat16)
    context = jnp.einsum('thqk,tkhc->tqhc', attention_probs.astype(jnp.float32), values_all)
    context = context.astype(jnp.bfloat16).reshape(text_count * L, D)
    first_norm = layer_norm(hidden_states.astype(jnp.float32) + jnp.dot(context, w_out, preferred_element_type=jnp.float32)).astype(jnp.bfloat16)
    inner_act = exact_gelu(jnp.dot(first_norm, w_up, preferred_element_type=jnp.float32)).astype(jnp.bfloat16)
    second_norm = layer_norm(first_norm.astype(jnp.float32) + jnp.dot(inner_act, w_down, preferred_element_type=jnp.float32))
    second_norm = second_norm.reshape(text_count, L, D)
    pooled = lax.optimization_barrier(jnp.sum(jnp.where(live_keys[:, :, None], second_norm, 0.0), axis=1)) / text_len[:, None].astype(jnp.float32)
    return pooled.astype(jnp.bfloat16)

def reference(hidden_states, text_len, w_qkv, w_out, w_up, w_down, hist, nbr, send_rows, fresh_target, w_self, w_neigh, upstream):
    fresh = encode(hidden_states, text_len, w_qkv, w_out, w_up, w_down)
    table = hist.at[fresh_target].set(fresh)
    blocks = table.reshape(N_DOM, G, D)
    sources = jnp.arange(N_DOM, dtype=jnp.int32)[:, None]

    def partition(grad_table, index):
        local_rows = blocks[index]
        wanted = send_rows[:, index, :]
        halo_block = jnp.where((wanted >= 0)[:, :, None], blocks[sources, jnp.maximum(wanted, 0)], jnp.zeros((), table.dtype))
        extended = jnp.concatenate([local_rows, halo_block.reshape(N_DOM * CAP, D)], axis=0)
        links = lax.dynamic_slice_in_dim(nbr, index * G, G, 0)
        total = jnp.zeros((G, D), jnp.float32)
        for neighbour in range(K):
            total = total + extended[links[:, neighbour]].astype(jnp.float32)
        agg_rows = (total / K).astype(jnp.bfloat16)
        pre_act = jnp.dot(local_rows, w_self, preferred_element_type=jnp.float32) + jnp.dot(agg_rows, w_neigh, preferred_element_type=jnp.float32)
        activated, pull_back = jax.vjp(exact_gelu, pre_act)
        cotangent = lax.dynamic_slice_in_dim(upstream, index * G, G, 0).astype(jnp.float32)
        grad_pre = pull_back(cotangent)[0].astype(jnp.bfloat16)
        grad_self = jnp.dot(grad_pre, w_self.T, preferred_element_type=jnp.float32)
        grad_total = jnp.dot(grad_pre, w_neigh.T, preferred_element_type=jnp.float32) / K
        grad_extended = jnp.zeros((G + N_DOM * CAP, D), jnp.float32)
        for neighbour in range(K):
            grad_extended = grad_extended.at[links[:, neighbour]].add(grad_total)
        grad_table = grad_table.at[index].add(grad_self + grad_extended[:G])
        target = jnp.where(wanted >= 0, wanted, G)
        grad_table = grad_table.at[sources, target].add(grad_extended[G:].reshape(N_DOM, CAP, D), mode='drop')
        return (grad_table, (activated.astype(jnp.bfloat16), agg_rows, grad_pre))
    start_grads = jnp.zeros((N_DOM, G, D), jnp.float32)
    grad_table, outputs = lax.scan(partition, start_grads, jnp.arange(N_DOM, dtype=jnp.int32))
    sage_out = outputs[0].reshape(NODES, D)
    agg_all = outputs[1].reshape(NODES, D)
    grad_all = outputs[2].reshape(NODES, D)
    grad_self_w = jnp.dot(table.T, grad_all, preferred_element_type=jnp.float32)
    grad_neigh_w = jnp.dot(agg_all.T, grad_all, preferred_element_type=jnp.float32)
    grad_fresh = grad_table.reshape(NODES, D)[fresh_target]
    return (sage_out, grad_fresh, grad_self_w, grad_neigh_w)
```

```python
import math

import jax
import jax.numpy as jnp
import numpy as np
from jax import lax
from jax.sharding import PartitionSpec as P

HEADS = 12
EPSILON = 1e-05
NX, NZ, NC, NY = 4, 8, 2, 4
BF = jnp.bfloat16
F32 = jnp.float32


def layer_norm(values):
    center = values - jnp.mean(values, axis=-1, keepdims=True)
    spread = jnp.mean(center * center, axis=-1, keepdims=True)
    return center * lax.rsqrt(spread + EPSILON)


def exact_gelu(values):
    return jax.nn.gelu(values, approximate=False)


def dot(a, b):
    return jnp.dot(a, b, preferred_element_type=F32)


def dot_t(a, b):
    return lax.dot_general(a, b, (((0,), (0,)), ((), ())), preferred_element_type=F32)


def dot_nt(a, b):
    return lax.dot_general(a, b, (((1,), (1,)), ((), ())), preferred_element_type=F32)


def pull(value, axis, shift):
    if axis == "y":
        return lax.ppermute(value, "mp", [((i + shift) % NY, i) for i in range(NY)])
    pairs = []
    for x in range(NX):
        for z in range(NZ):
            for c in range(NC):
                sx, sz, sc = x, z, c
                if axis == "x":
                    sx = (x + shift) % NX
                elif axis == "z":
                    sz = (z + shift) % NZ
                else:
                    sc = (c + shift) % NC
                pairs.append(((sx * NZ + sz) * NC + sc, (x * NZ + z) * NC + c))
    return lax.ppermute(value, "dom", pairs)


def flip(value, axis, bit):
    scale = {"c": 1, "z": NC, "x": NC * NZ}[axis] * bit
    count = NX * NZ * NC
    return lax.ppermute(value, "dom", [(i, i ^ scale) for i in range(count)])


def attend(rows, lengths, weights_qkv):
    model_width = rows.shape[1]
    text_count = lengths.shape[0]
    length = rows.shape[0] // text_count
    local_width = weights_qkv.shape[2]
    head_dim = model_width // HEADS
    head_count = local_width // head_dim
    packed = dot(rows, weights_qkv.reshape(model_width, 3 * local_width)).astype(BF)
    packed = packed.reshape(text_count, length, 3, head_count, head_dim)
    scores = jnp.einsum(
        "tqhc,tkhc->thqk", packed[:, :, 0], packed[:, :, 1], preferred_element_type=F32
    ) / math.sqrt(head_dim)
    live_keys = jnp.arange(length)[None, :] < lengths[:, None]
    scores = jnp.where(live_keys[:, None, None, :], scores, -1e30)
    row_peak = jnp.max(scores, axis=-1, keepdims=True)
    weights = jnp.exp(scores - row_peak)
    attention_probs = (weights / jnp.sum(weights, axis=-1, keepdims=True)).astype(BF)
    context = jnp.einsum(
        "thqk,tkhc->tqhc", attention_probs, packed[:, :, 2], preferred_element_type=F32
    )
    return context.astype(BF).reshape(text_count * length, local_width)


def encode_block(hidden_states, text_len, w_qkv, w_out, w_up, w_down):
    model_width = hidden_states.shape[1]
    length = hidden_states.shape[0] // NY
    me = lax.axis_index("mp")
    own_len = lax.dynamic_index_in_dim(text_len, me, 0, keepdims=False)
    texts = hidden_states.reshape(NY, length, model_width)
    residual = lax.dynamic_index_in_dim(texts, me, 0, keepdims=False)
    context = attend(hidden_states, text_len, w_qkv)
    attended = dot(context, w_out).astype(BF).reshape(NY, length, model_width)

    def part(s):
        return lax.dynamic_index_in_dim(attended, (me + s) % NY, 0, keepdims=False)

    total = residual.astype(F32) + part(0).astype(F32)
    for s in (1, 3, 2):
        total = total + pull(part(NY - s), "y", s).astype(F32)
    first_norm = layer_norm(total).astype(BF)

    def feed(block):
        return dot(exact_gelu(dot(block, w_up)).astype(BF), w_down)

    others = {s: pull(first_norm, "y", s) for s in (1, 3, 2)}
    summed = first_norm.astype(F32) + feed(first_norm)
    for s in (1, 3, 2):
        summed = summed + pull(feed(others[s]).astype(BF), "y", NY - s).astype(F32)
    second_norm = layer_norm(summed)
    own_live = jnp.arange(length) < own_len
    pooled = jnp.sum(jnp.where(own_live[:, None], second_norm, 0.0), axis=0, keepdims=True)
    return (pooled / own_len.astype(F32)).astype(BF)


GATHER_STAGES = (("y", (1, 3, 2)), ("z", (1, 2, 3)), ("z", (4,)), ("x", (1, 3, 2)), ("c", (1,)))


def slot_offsets():
    offsets = {axis: np.zeros((1,), np.int32) for axis in "xzcy"}
    for axis, shifts in GATHER_STAGES:
        offsets = {
            other: np.concatenate(
                [values] + [values + (s if other == axis else 0) for s in shifts]
            )
            for other, values in offsets.items()
        }
    return offsets


def gather_fresh(row):
    for axis, shifts in GATHER_STAGES:
        row = jnp.concatenate([row] + [pull(row, axis, s) for s in shifts], axis=0)
    return row


def reduce_dom(parts, dom):
    block = parts.shape[1:]
    parts = parts.reshape((2,) * 6 + block)
    names = [("x", 2), ("x", 1), ("z", 4), ("z", 2), ("z", 1), ("c", 1)]
    shift = {("x", 2): 5, ("x", 1): 4, ("z", 4): 3, ("z", 2): 2, ("z", 1): 1, ("c", 1): 0}
    for name in (("c", 1), ("z", 1), ("x", 1), ("z", 2), ("x", 2), ("z", 4)):
        place = names.index(name)
        names.pop(place)
        parts = jnp.moveaxis(parts, place, 0)
        bit = (dom >> shift[name]) & 1
        keep = lax.dynamic_index_in_dim(parts, bit, 0, keepdims=False)
        send = lax.dynamic_index_in_dim(parts, 1 - bit, 0, keepdims=False)
        parts = keep.astype(F32) + flip(send.astype(BF), *name).astype(F32)
    return parts


def local(
    hidden_states,
    text_len,
    w_qkv,
    w_out,
    w_up,
    w_down,
    hist,
    nbr,
    send_rows,
    fresh_target,
    w_self,
    w_neigh,
    upstream,
):
    dom = lax.axis_index("dom")
    mp = lax.axis_index("mp")
    node_count, model_width = hist.shape
    text_count = fresh_target.shape[0]
    quarter = w_self.shape[1]
    peer_count, slot_count = send_rows.shape[1:]
    fanout = nbr.shape[1]

    offsets = slot_offsets()
    my_c, my_z, my_x = dom % NC, (dom // NC) % NZ, dom // (NC * NZ)
    slot_dom = (
        ((my_x + offsets["x"]) % NX) * (NZ * NC)
        + ((my_z + offsets["z"]) % NZ) * NC
        + (my_c + offsets["c"]) % NC
    )
    slot_text = slot_dom * NY + (mp + offsets["y"]) % NY
    text_ids = jnp.arange(text_count, dtype=jnp.int32)

    target_row = fresh_target - dom * node_count
    row_ids = jnp.arange(node_count, dtype=jnp.int32)
    holds = row_ids[:, None] == target_row[None, :]
    replaced = jnp.any(holds, axis=1)
    row_text = jnp.sum(jnp.where(holds, text_ids[None, :], 0), axis=1)
    column = jnp.arange(model_width, dtype=jnp.int32)[None, :]
    code = jnp.where(
        column == 0,
        32 + row_text[:, None] // 16,
        jnp.where(column == 1, 32 + row_text[:, None] % 16, 0),
    ).astype(BF)
    coded = jnp.where(replaced[:, None], code, hist)
    base = jnp.where(replaced[:, None], jnp.zeros((), BF), hist)
    wanted = send_rows[0].reshape(peer_count * slot_count)
    pick = (wanted[:, None] == row_ids[None, :]).astype(BF)
    outgoing = dot(pick, coded).astype(BF).reshape(peer_count, slot_count, model_width)
    received = lax.all_to_all(outgoing, "dom", split_axis=0, concat_axis=0, tiled=True)
    received = received.reshape(peer_count * slot_count, model_width)
    is_text = received[:, 0] > 24
    halo_text = ((received[:, 0].astype(F32) - 32) * 16 + received[:, 1].astype(F32) - 32).astype(
        jnp.int32
    )
    halo_text = jnp.where(is_text, halo_text, -1)
    halo = jnp.where(is_text[:, None], jnp.zeros((), BF), received)
    row_text = jnp.where(replaced, row_text, -1)
    extended_text = jnp.concatenate([row_text, halo_text])
    extended_ids = jnp.arange(extended_text.shape[0], dtype=jnp.int32)
    counts = jnp.zeros((node_count, extended_text.shape[0]), F32)
    for neighbour in range(fanout):
        counts = counts + (nbr[:, neighbour : neighbour + 1] == extended_ids[None, :]).astype(F32)
    counts = counts.astype(BF)
    agg_base = dot(counts[:, :node_count], base) + dot(counts[:, node_count:], halo)
    by_slot = (extended_text[:, None] == slot_text[None, :]).astype(BF)
    by_text = (extended_text[:, None] == text_ids[None, :]).astype(BF)
    counts_slot = dot(counts, by_slot).astype(BF)
    counts_text = dot(counts, by_text).astype(BF)
    place_slot = by_slot[:node_count]
    place_text = by_text[:node_count]

    fresh_row = encode_block(hidden_states, text_len, w_qkv, w_out, w_up, w_down)
    fresh = gather_fresh(fresh_row)

    table = base + dot(place_slot, fresh).astype(BF)
    agg_rows = ((agg_base + dot(counts_slot, fresh)) / fanout).astype(BF)
    pre_act = dot(table, w_self) + dot(agg_rows, w_neigh)
    activated, pull_back = jax.vjp(exact_gelu, pre_act)
    sage_out = activated.astype(BF)
    grad_pre = pull_back(upstream.astype(F32))[0].astype(BF)
    weight_parts = jnp.concatenate([dot_t(table, grad_pre), dot_t(agg_rows, grad_pre)], axis=1)
    text_parts = jnp.concatenate(
        [dot_t(place_text, grad_pre), dot_t(counts_text, grad_pre) / fanout], axis=1
    )
    share = model_width // peer_count
    own_texts = text_count // peer_count
    parts = jnp.concatenate(
        [
            weight_parts.reshape(peer_count, share, 2 * quarter),
            text_parts.reshape(peer_count, own_texts, 2 * quarter),
        ],
        axis=1,
    )
    reduced = reduce_dom(parts, dom)
    grad_self_w = reduced[:share, :quarter]
    grad_neigh_w = reduced[:share, quarter:]
    rows = reduced[share:].astype(BF)
    terms = dot_nt(rows[:, :quarter], w_self) + dot_nt(rows[:, quarter:], w_neigh)
    terms = terms.reshape(own_texts, NY, quarter)

    def term(s):
        return lax.dynamic_index_in_dim(terms, (mp + s) % NY, 1, keepdims=False)

    grad_fresh = term(0)
    for s in (1, 3, 2):
        grad_fresh = grad_fresh + pull(term(NY - s), "y", s)
    return (sage_out, grad_fresh, grad_self_w, grad_neigh_w)


def solution(mesh):
    in_specs = (
        P("dom", None),
        P("dom"),
        P(None, None, "mp"),
        P("mp", None),
        P(None, "mp"),
        P("mp", None),
        P("dom", None),
        P("dom", None),
        P("dom", None, None),
        P(),
        P(None, "mp"),
        P(None, "mp"),
        P("dom", "mp"),
    )
    out_specs = (P("dom", "mp"), P("dom", "mp"), P("dom", "mp"), P("dom", "mp"))
    return jax.shard_map(local, mesh=mesh, in_specs=in_specs, out_specs=out_specs, check_vma=False)
```

```python
import math

import jax
import jax.numpy as jnp
import numpy as np
from jax import lax
from jax.experimental import pallas as pl
from jax.experimental.pallas import tpu as pltpu
from jax.sharding import Mesh, PartitionSpec as P

HEADS = 12
EPSILON = 1e-05
NX, NZ, NC, NY = 4, 8, 2, 4
BF = jnp.bfloat16
F32 = jnp.float32


def layer_norm(values):
    center = values - jnp.mean(values, axis=-1, keepdims=True)
    spread = jnp.mean(center * center, axis=-1, keepdims=True)
    return center * lax.rsqrt(spread + EPSILON)


def exact_gelu(values):
    return 0.5 * values * (1.0 + lax.erf(values * math.sqrt(0.5)))


def dot(a, b):
    return jnp.dot(a, b, preferred_element_type=F32)


def dot_t(a, b):
    return lax.dot_general(a, b, (((0,), (0,)), ((), ())), preferred_element_type=F32)


def dot_nt(a, b):
    return lax.dot_general(a, b, (((1,), (1,)), ((), ())), preferred_element_type=F32)


def pull(value, axis, shift):
    count = {"x": NX, "z": NZ, "c": NC, "y": NY}[axis]
    return lax.ppermute(value, axis, [((i + shift) % count, i) for i in range(count)])


def attend(rows, lengths, weights_qkv):
    model_width = rows.shape[1]
    text_count = lengths.shape[0]
    length = rows.shape[0] // text_count
    local_width = weights_qkv.shape[2]
    head_dim = model_width // HEADS
    head_count = local_width // head_dim
    packed = dot(rows, weights_qkv.reshape(model_width, 3 * local_width)).astype(BF)
    packed = packed.reshape(text_count, length, 3, head_count, head_dim)
    scores = jnp.einsum(
        "tqhc,tkhc->thqk", packed[:, :, 0], packed[:, :, 1], preferred_element_type=F32
    ) / math.sqrt(head_dim)
    live_keys = jnp.arange(length)[None, :] < lengths[:, None]
    scores = jnp.where(live_keys[:, None, None, :], scores, -1e30)
    row_peak = jnp.max(scores, axis=-1, keepdims=True)
    weights = jnp.exp(scores - row_peak)
    attention_probs = (weights / jnp.sum(weights, axis=-1, keepdims=True)).astype(BF)
    context = jnp.einsum(
        "thqk,tkhc->tqhc", attention_probs, packed[:, :, 2], preferred_element_type=F32
    )
    return context.astype(BF).reshape(text_count * length, local_width)


def encode_block(hidden_states, text_len, w_qkv, w_out, w_up, w_down):
    model_width = hidden_states.shape[1]
    length = hidden_states.shape[0] // NY
    me = lax.axis_index("y")
    own_len = lax.dynamic_index_in_dim(text_len, me, 0, keepdims=False)
    texts = hidden_states.reshape(NY, length, model_width)
    residual = lax.dynamic_index_in_dim(texts, me, 0, keepdims=False)
    context = attend(hidden_states, text_len, w_qkv)
    attended = dot(context, w_out).astype(BF).reshape(NY, length, model_width)

    def part(s):
        return lax.dynamic_index_in_dim(attended, (me + s) % NY, 0, keepdims=False)

    total = residual.astype(F32) + part(0).astype(F32)
    for s in (1, 3, 2):
        total = total + pull(part(NY - s), "y", s).astype(F32)
    first_norm = layer_norm(total).astype(BF)

    def feed(block):
        return dot(exact_gelu(dot(block, w_up)).astype(BF), w_down)

    others = {s: pull(first_norm, "y", s) for s in (1, 3, 2)}
    summed = first_norm.astype(F32) + feed(first_norm)
    for s in (1, 3, 2):
        summed = summed + pull(feed(others[s]).astype(BF), "y", NY - s).astype(F32)
    second_norm = layer_norm(summed)
    own_live = jnp.arange(length) < own_len
    pooled = jnp.sum(jnp.where(own_live[:, None], second_norm, 0.0), axis=0, keepdims=True)
    return (pooled / own_len.astype(F32)).astype(BF)


def whole(count):
    return [pl.BlockSpec(memory_space=pltpu.VMEM)] * count


def places(peer_count, share, own_texts):
    block = share + own_texts
    rows = np.zeros((NC, peer_count * share, peer_count // NC * block), np.float32)
    texts = np.zeros((NC, peer_count * own_texts, peer_count // NC * block), np.float32)
    for d in range(peer_count):
        chip, core = d // NC, d % NC
        for i in range(share):
            rows[core, d * share + i, chip * block + i] = 1
        for i in range(own_texts):
            texts[core, d * own_texts + i, chip * block + share + i] = 1
    return rows.astype(jnp.bfloat16), texts.astype(jnp.bfloat16)


def outgoing_kernel(target_ref, wanted_ref, hist_ref, out_ref, base_ref, place_ref, row_text_ref):
    count, width = hist_ref.shape
    texts = target_ref.shape[1]
    row_ids = lax.broadcasted_iota(jnp.int32, (count, texts), 0)
    text_ids = lax.broadcasted_iota(jnp.int32, (count, texts), 1)
    holds = row_ids == target_ref[...]
    row_text = jnp.sum(jnp.where(holds, text_ids + 1, 0), axis=1, keepdims=True) - 1
    replaced = row_text >= 0
    column = lax.broadcasted_iota(jnp.int32, (count, width), 1)
    code = jnp.where(
        column == 0, 32 + row_text // 16, jnp.where(column == 1, 32 + row_text % 16, 0)
    ).astype(F32)
    hist = hist_ref[...].astype(F32)
    base_ref[...] = jnp.where(replaced, 0.0, hist).astype(BF)
    place_ref[...] = holds.astype(F32).astype(BF)
    row_text_ref[...] = row_text
    coded = jnp.where(replaced, code, hist).astype(BF)
    ids = lax.broadcasted_iota(jnp.int32, (wanted_ref.shape[0], count), 1)
    pick = (wanted_ref[...] == ids).astype(F32).astype(BF)
    out_ref[...] = dot(pick, coded).astype(BF)


def outgoing_rows(target_row, wanted, hist):
    count, width = hist.shape
    return pl.pallas_call(
        outgoing_kernel,
        out_shape=(
            jax.ShapeDtypeStruct((wanted.shape[0], width), BF),
            jax.ShapeDtypeStruct((count, width), BF),
            jax.ShapeDtypeStruct((count, target_row.shape[1]), BF),
            jax.ShapeDtypeStruct((count, 1), jnp.int32),
        ),
        in_specs=whole(3),
        out_specs=tuple(whole(4)),
        compiler_params=pltpu.CompilerParams(vmem_limit_bytes=48 * 2**20),
        cost_estimate=pl.CostEstimate(flops=400000000, bytes_accessed=3000000, transcendentals=0),
        name="outgoing_rows",
    )(target_row, wanted, hist)


def halo_kernel(
    received_ref,
    base_ref,
    nbr_ref,
    place_ref,
    row_text_ref,
    slot_ref,
    text_place_ref,
    agg_ref,
    counts_slot_ref,
    place_slot_ref,
    place_text_ref,
    counts_text_ref,
):
    count, fanout = nbr_ref.shape
    texts = place_ref.shape[1]
    received = received_ref[...].astype(F32)
    is_text = received[:, 0:1] > 24
    halo_text = ((received[:, 0:1] - 32) * 16 + received[:, 1:2] - 32).astype(jnp.int32)
    halo_text = jnp.where(is_text, halo_text, -1)
    halo = jnp.where(is_text, 0.0, received).astype(BF)
    size = received.shape[0]
    local_ids = lax.broadcasted_iota(jnp.int32, (count, count), 1)
    halo_ids = lax.broadcasted_iota(jnp.int32, (count, size), 1) + count
    near = jnp.zeros((count, count), F32)
    far = jnp.zeros((count, size), F32)
    for neighbour in range(fanout):
        link = nbr_ref[:, neighbour : neighbour + 1]
        near = near + (link == local_ids).astype(F32)
        far = far + (link == halo_ids).astype(F32)
    near = near.astype(BF)
    far = far.astype(BF)
    agg_ref[...] = dot(near, base_ref[...]) + dot(far, halo)
    slots = slot_ref[...]
    text_ids = lax.broadcasted_iota(jnp.int32, (1, texts), 1)
    place = place_ref[...]
    place_slot = (row_text_ref[...] == slots).astype(F32).astype(BF)
    halo_slot = (halo_text == slots).astype(F32).astype(BF)
    halo_place = (halo_text == text_ids).astype(F32).astype(BF)
    place_slot_ref[...] = place_slot
    counts_slot_ref[...] = (dot(near, place_slot) + dot(far, halo_slot)).astype(BF)
    counts_text = (dot(near, place) + dot(far, halo_place)).astype(BF)
    for core in range(NC):
        place_text_ref[core] = dot(place, text_place_ref[core]).astype(BF)
        counts_text_ref[core] = dot(counts_text, text_place_ref[core]).astype(BF)


def halo_sums(received, base, nbr, place, row_text, slots, text_place):
    count, width = base.shape
    texts = place.shape[1]
    half = jax.ShapeDtypeStruct((NC, count, text_place.shape[2]), BF)
    return pl.pallas_call(
        halo_kernel,
        out_shape=(
            jax.ShapeDtypeStruct((count, width), F32),
            jax.ShapeDtypeStruct((count, texts), BF),
            jax.ShapeDtypeStruct((count, texts), BF),
            half,
            half,
        ),
        in_specs=whole(7),
        out_specs=tuple(whole(5)),
        compiler_params=pltpu.CompilerParams(vmem_limit_bytes=48 * 2**20),
        cost_estimate=pl.CostEstimate(flops=1500000000, bytes_accessed=5000000, transcendentals=0),
        name="halo_sums",
    )(received, base, nbr, place, row_text, slots, text_place)


def sage_kernel(
    fanout,
    core_ref,
    fresh_ref,
    other_ref,
    base_ref,
    agg_base_ref,
    counts_slot_ref,
    place_slot_ref,
    place_text_ref,
    counts_text_ref,
    row_place_ref,
    w_self_ref,
    w_neigh_ref,
    upstream_ref,
    sage_ref,
    keep_ref,
    send_ref,
):
    core = core_ref[0]
    half = fresh_ref.shape[0]
    quarter = w_self_ref.shape[1]
    fresh, other = fresh_ref[...], other_ref[...]
    placed = dot(place_slot_ref[:, :half], fresh) + dot(place_slot_ref[:, half:], other)
    table = base_ref[...] + placed.astype(BF)
    added = dot(counts_slot_ref[:, :half], fresh) + dot(counts_slot_ref[:, half:], other)
    agg_rows = ((agg_base_ref[...] + added) / fanout).astype(BF)
    pre_act = dot(table, w_self_ref[...]) + dot(agg_rows, w_neigh_ref[...])
    cdf = 0.5 * (1.0 + lax.erf(pre_act * math.sqrt(0.5)))
    density = jnp.exp(-0.5 * pre_act * pre_act) * (1.0 / math.sqrt(2.0 * math.pi))
    sage_ref[...] = (pre_act * cdf).astype(BF)
    grad_pre = (upstream_ref[...].astype(F32) * (cdf + pre_act * density)).astype(BF)
    for side, out_ref in ((core, keep_ref), (1 - core, send_ref)):
        row_place = row_place_ref[side]
        left = dot(table, row_place).astype(BF) + place_text_ref[side]
        out_ref[:, :quarter] = dot_t(left, grad_pre).astype(BF)
        left = dot(agg_rows, row_place).astype(BF) + counts_text_ref[side]
        out_ref[:, quarter:] = dot_t(left, grad_pre).astype(BF)


def sage(core, fresh, other, halo_parts, base, row_place, w_self, w_neigh, upstream, fanout):
    agg_base, counts_slot, place_slot, place_text, counts_text = halo_parts
    block = jax.ShapeDtypeStruct((place_text.shape[2], 2 * w_self.shape[1]), BF)
    return pl.pallas_call(
        lambda *refs: sage_kernel(fanout, *refs),
        out_shape=(jax.ShapeDtypeStruct(upstream.shape, BF), block, block),
        in_specs=[pl.BlockSpec(memory_space=pltpu.SMEM)] + whole(12),
        out_specs=tuple(whole(3)),
        compiler_params=pltpu.CompilerParams(vmem_limit_bytes=48 * 2**20),
        cost_estimate=pl.CostEstimate(flops=1500000000, bytes_accessed=8000000, transcendentals=0),
        name="sage",
    )(
        core,
        fresh,
        other,
        base,
        agg_base,
        counts_slot,
        place_slot,
        place_text,
        counts_text,
        row_place,
        w_self,
        w_neigh,
        upstream,
    )


def local(
    hidden_states,
    text_len,
    w_qkv,
    w_out,
    w_up,
    w_down,
    hist,
    nbr,
    send_rows,
    fresh_target,
    w_self,
    w_neigh,
    upstream,
):
    my_x, my_z, my_c, mp = (lax.axis_index(axis) for axis in "xzcy")
    dom = (my_x * NZ + my_z) * NC + my_c
    node_count, model_width = hist.shape
    text_count = fresh_target.shape[0]
    quarter = w_self.shape[1]
    peer_count, slot_count = send_rows.shape[1:]
    fanout = nbr.shape[1]
    share = model_width // peer_count
    own_texts = text_count // peer_count
    chips = peer_count // NC

    order = np.arange(text_count)
    slot_core = (order // (chips * NY) + my_c) % NC
    slot_y = (np.array([0, 1, 3, 2])[order % NY] + mp) % NY
    slot_text = (((order // NY % chips) * NC + slot_core) * NY + slot_y).astype(jnp.int32)
    row_place, text_place = places(peer_count, share, own_texts)

    target_row = (fresh_target - dom * node_count)[None, :]
    wanted = send_rows.reshape(peer_count * slot_count, 1)
    outgoing, base, place, row_text = outgoing_rows(target_row, wanted, hist)
    received = lax.all_to_all(
        outgoing.reshape(peer_count, slot_count, model_width),
        ("x", "z", "c"),
        split_axis=0,
        concat_axis=0,
        tiled=True,
    )
    halo_parts = halo_sums(
        received.reshape(peer_count * slot_count, model_width),
        base,
        nbr,
        place,
        row_text,
        slot_text[None, :],
        jnp.asarray(text_place),
    )

    fresh_row = encode_block(hidden_states, text_len, w_qkv, w_out, w_up, w_down)
    fresh_row, halo_parts = lax.optimization_barrier((fresh_row, halo_parts))
    rows = jnp.concatenate([fresh_row] + [pull(fresh_row, "y", s) for s in (1, 3, 2)], axis=0)
    rows = jnp.broadcast_to(rows[None], (chips,) + rows.shape)
    fresh = lax.all_to_all(rows, ("x", "z"), split_axis=0, concat_axis=0, tiled=True)
    fresh = fresh.reshape(chips * NY, model_width)
    other = pull(fresh, "c", 1)

    sage_out, keep, send = sage(
        my_c.reshape(1),
        fresh,
        other,
        halo_parts,
        base,
        jnp.asarray(row_place),
        w_self,
        w_neigh,
        upstream,
        fanout,
    )
    parts = (keep.astype(F32) + pull(send, "c", 1).astype(F32)).astype(BF)
    parts = parts.reshape(chips, share + own_texts, 2 * quarter)
    parts = lax.all_to_all(parts, ("x", "z"), split_axis=0, concat_axis=0, tiled=True)
    reduced = jnp.sum(parts.astype(F32), axis=0)
    grad_self_w = reduced[:share, :quarter]
    grad_neigh_w = reduced[:share, quarter:]
    rows = reduced[share:].astype(BF)
    terms = dot_nt(rows[:, :quarter], w_self) + dot_nt(rows[:, quarter:], w_neigh) / fanout
    terms = terms.reshape(own_texts, NY, quarter)

    def term(s):
        return lax.dynamic_index_in_dim(terms, (mp + s) % NY, 1, keepdims=False)

    grad_fresh = term(0)
    for s in (1, 3, 2):
        grad_fresh = grad_fresh + pull(term(NY - s), "y", s)
    return (sage_out, grad_fresh, grad_self_w, grad_neigh_w)


def solution(mesh):
    dom = ("x", "z", "c")
    split = Mesh(mesh.devices.reshape(NX, NZ, NC, NY), dom + ("y",))
    in_specs = (
        P(dom, None),
        P(dom),
        P(None, None, "y"),
        P("y", None),
        P(None, "y"),
        P("y", None),
        P(dom, None),
        P(dom, None),
        P(dom, None, None),
        P(),
        P(None, "y"),
        P(None, "y"),
        P(dom, "y"),
    )
    out_specs = (P(dom, "y"),) * 4
    return jax.shard_map(local, mesh=split, in_specs=in_specs, out_specs=out_specs, check_vma=False)
```

```python
import math

import jax
import jax.numpy as jnp
from jax import lax
from jax.experimental import pallas as pl
from jax.experimental.pallas import tpu as pltpu
from jax.sharding import Mesh, PartitionSpec as P

HEADS = 12
EPSILON = 1e-05
NX, NZ, NC, NY = 4, 8, 2, 4
BF = jnp.bfloat16
F32 = jnp.float32


def layer_norm(values):
    center = values - jnp.mean(values, axis=-1, keepdims=True)
    spread = jnp.mean(center * center, axis=-1, keepdims=True)
    return center * lax.rsqrt(spread + EPSILON)


def exact_gelu(values):
    return 0.5 * values * (1.0 + lax.erf(values * math.sqrt(0.5)))


def dot(a, b):
    return jnp.dot(a, b, preferred_element_type=F32)


def dot_t(a, b):
    return lax.dot_general(a, b, (((0,), (0,)), ((), ())), preferred_element_type=F32)


def dot_nt(a, b):
    return lax.dot_general(a, b, (((1,), (1,)), ((), ())), preferred_element_type=F32)


def pull(value, axis, shift):
    count = {"x": NX, "z": NZ, "c": NC, "y": NY}[axis]
    return lax.ppermute(value, axis, [((i + shift) % count, i) for i in range(count)])


def whole(count):
    return [pl.BlockSpec(memory_space=pltpu.VMEM)] * count


def far_off(count):
    return [pl.BlockSpec(memory_space=pltpu.HBM)] * count


def scalars():
    return [pl.BlockSpec(memory_space=pltpu.SMEM)]


def grant(mib, flops, bytes_accessed):
    return {
        "compiler_params": pltpu.CompilerParams(vmem_limit_bytes=mib * 2**20),
        "cost_estimate": pl.CostEstimate(
            flops=flops, bytes_accessed=bytes_accessed, transcendentals=0
        ),
    }


def room(*arrays):
    return [pltpu.VMEM(a.shape, a.dtype) for a in arrays] + [pltpu.SemaphoreType.DMA((len(arrays),))]


def fetch(sources, targets, semaphores):
    copies = [
        pltpu.make_async_copy(source, target, semaphores.at[k])
        for k, (source, target) in enumerate(zip(sources, targets))
    ]
    for copy in copies:
        copy.start()
    return copies


DOM, CORE, ME, LENGTHS = 0, 1, 2, 3


def attend(rows, lengths, weights_qkv):
    model_width = rows.shape[1]
    text_count = lengths.shape[0]
    length = rows.shape[0] // text_count
    local_width = weights_qkv.shape[2]
    head_dim = model_width // HEADS
    head_count = local_width // head_dim
    packed = dot(rows, weights_qkv.reshape(model_width, 3 * local_width)).astype(BF)
    packed = packed.reshape(text_count, length, 3, head_count, head_dim)
    scores = jnp.einsum(
        "tqhc,tkhc->thqk", packed[:, :, 0], packed[:, :, 1], preferred_element_type=F32
    ) / math.sqrt(head_dim)
    live_keys = jnp.arange(length)[None, :] < lengths[:, None]
    scores = jnp.where(live_keys[:, None, None, :], scores, -1e30)
    row_peak = jnp.max(scores, axis=-1, keepdims=True)
    weights = jnp.exp(scores - row_peak)
    attention_probs = (weights / jnp.sum(weights, axis=-1, keepdims=True)).astype(BF)
    context = jnp.einsum(
        "thqk,tkhc->tqhc", attention_probs, packed[:, :, 2], preferred_element_type=F32
    )
    return context.astype(BF).reshape(text_count * length, local_width)


def norm_kernel(residual_ref, own_ref, near_ref, far_ref, across_ref, out_ref):
    total = residual_ref[...].astype(F32) + own_ref[...].astype(F32)
    for ref in (near_ref, far_ref, across_ref):
        total = total + ref[...].astype(F32)
    out_ref[...] = layer_norm(total).astype(BF)


def first_layer_norm(residual, parts):
    return pl.pallas_call(
        norm_kernel,
        out_shape=jax.ShapeDtypeStruct(residual.shape, BF),
        in_specs=whole(5),
        out_specs=whole(1)[0],
        name="first_norm",
        **grant(16, 4000000000, 1200000),
    )(residual, *parts)


def feed_kernel(block_ref, up_ref, down_ref, out_ref):
    inner = exact_gelu(dot(block_ref[...], up_ref[...])).astype(BF)
    out_ref[...] = dot(inner, down_ref[...]).astype(out_ref.dtype)


def feed_first_kernel(block_ref, up_hbm, down_hbm, out_ref, up_ref, down_ref, semaphores):
    copies = fetch((up_hbm, down_hbm), (up_ref, down_ref), semaphores)
    copies[0].wait()
    inner = exact_gelu(dot(block_ref[...], up_ref[...])).astype(BF)
    copies[1].wait()
    out_ref[...] = dot(inner, down_ref[...])


def feed_first(block, w_up, w_down):
    return pl.pallas_call(
        feed_first_kernel,
        out_shape=(
            jax.ShapeDtypeStruct(block.shape, F32),
            jax.ShapeDtypeStruct(w_up.shape, BF),
            jax.ShapeDtypeStruct(w_down.shape, BF),
        ),
        in_specs=whole(1) + far_off(2),
        out_specs=tuple(whole(3)),
        scratch_shapes=[pltpu.SemaphoreType.DMA((2,))],
        name="feed_first",
        **grant(16, 8000000000, 9000000),
    )(block, w_up, w_down)


def feed(block, w_up, w_down):
    return pl.pallas_call(
        feed_kernel,
        out_shape=jax.ShapeDtypeStruct(block.shape, BF),
        in_specs=whole(3),
        out_specs=whole(1)[0],
        name="feed",
        **grant(16, 8000000000, 9000000),
    )(block, w_up, w_down)


def pool_kernel(place_ref, first_ref, own_ref, near_ref, far_ref, across_ref, out_ref):
    total = first_ref[...].astype(F32) + own_ref[...]
    for ref in (near_ref, far_ref, across_ref):
        total = total + ref[...].astype(F32)
    normed = layer_norm(total)
    length = place_ref[LENGTHS + place_ref[ME]]
    live = lax.broadcasted_iota(jnp.int32, normed.shape, 0) < length
    pooled = jnp.sum(jnp.where(live, normed, 0.0), axis=0, keepdims=True)
    out_ref[...] = (pooled / length.astype(F32)).astype(BF)


def pooled_row(place, first_norm, parts):
    return pl.pallas_call(
        pool_kernel,
        out_shape=jax.ShapeDtypeStruct((1, first_norm.shape[1]), BF),
        in_specs=scalars() + whole(5),
        out_specs=whole(1)[0],
        name="pooled_row",
        **grant(16, 4000000000, 1200000),
    )(place, first_norm, *parts)


def spread_kernel(own_ref, near_ref, far_ref, across_ref, out_ref):
    refs = (own_ref, near_ref, far_ref, across_ref)
    index = lax.broadcasted_iota(jnp.int32, out_ref.shape[1:], 0)
    rows = jnp.zeros(out_ref.shape[1:], F32)
    for s, ref in enumerate(refs):
        rows = jnp.where(index == s, ref[...].astype(F32), rows)
    out_ref[...] = jnp.broadcast_to(rows.astype(BF)[None], out_ref.shape)


def spread_rows(rows, chips):
    return pl.pallas_call(
        spread_kernel,
        out_shape=jax.ShapeDtypeStruct((chips, len(rows), rows[0].shape[1]), BF),
        in_specs=whole(len(rows)),
        out_specs=whole(1)[0],
        name="spread_rows",
        **grant(16, 1000000, 200000),
    )(*rows)


def sliced(values, index, width):
    total = values[:, :width]
    for k in range(1, values.shape[1] // width):
        total = jnp.where(index == k, values[:, k * width : (k + 1) * width], total)
    return total


def text_rows(target, count, dom):
    shape = (count, target.shape[1])
    row_ids = lax.broadcasted_iota(jnp.int32, shape, 0) + dom * count
    text_ids = lax.broadcasted_iota(jnp.int32, shape, 1)
    holds = row_ids == target
    row_text = jnp.sum(jnp.where(holds, text_ids + 1, 0), axis=1, keepdims=True) - 1
    return holds.astype(F32).astype(BF), row_text


def slot_texts(texts, chips, core, me):
    slot = lax.broadcasted_iota(jnp.int32, (1, texts), 1)
    step = slot % NY
    slot_y = ((step ^ (step >> 1)) + me) % NY
    slot_core = (slot // (chips * NY) + core) % NC
    return ((slot // NY % chips) * NC + slot_core) * NY + slot_y


def outgoing_kernel(place_ref, target_ref, wanted_ref, hist_hbm, out_ref, hist_ref, semaphores):
    copies = fetch((hist_hbm,), (hist_ref,), semaphores)
    count, width = hist_ref.shape
    _, row_text = text_rows(target_ref[...], count, place_ref[DOM])
    column = lax.broadcasted_iota(jnp.int32, (count, width), 1)
    code = jnp.where(
        column == 0, 32 + row_text // 16, jnp.where(column == 1, 32 + row_text % 16, 0)
    ).astype(F32)
    ids = lax.broadcasted_iota(jnp.int32, (wanted_ref.shape[0], count), 1)
    pick = (wanted_ref[...] == ids).astype(F32).astype(BF)
    copies[0].wait()
    coded = jnp.where(row_text >= 0, code, hist_ref[...].astype(F32)).astype(BF)
    out_ref[...] = dot(pick, coded).astype(BF).reshape(out_ref.shape)


def outgoing_rows(place, target, wanted, hist, chips):
    rows, width = wanted.shape[0], hist.shape[1]
    return pl.pallas_call(
        outgoing_kernel,
        out_shape=jax.ShapeDtypeStruct((chips, NC, rows // chips // NC, width), BF),
        in_specs=scalars() + whole(2) + far_off(1),
        out_specs=pl.BlockSpec(),
        scratch_shapes=room(hist),
        name="outgoing_rows",
        **grant(52, 2000000000, 6000000),
    )(place, target, wanted, hist)


def halo_kernel(
    place_ref,
    target_hbm,
    links_hbm,
    hist_hbm,
    received_hbm,
    across_hbm,
    sum_ref,
    counts_slot_ref,
    counts_text_ref,
    target_ref,
    links_ref,
    hist_ref,
    received_ref,
    across_ref,
    semaphores,
):
    copies = fetch(
        (target_hbm, links_hbm, hist_hbm, received_hbm, across_hbm),
        (target_ref, links_ref, hist_ref, received_ref, across_ref),
        semaphores,
    )
    chips, slot_count, width = across_ref.shape
    size = chips * slot_count
    fanout, count = links_ref.shape
    texts = target_ref.shape[1]
    core, me = place_ref[CORE], place_ref[ME]
    slots = slot_texts(texts, chips, core, me)
    text_ids = lax.broadcasted_iota(jnp.int32, slots.shape, 1)
    copies[0].wait()
    copies[1].wait()
    place, row_text = text_rows(target_ref[...], count, place_ref[DOM])

    def counted(ids):
        total = jnp.zeros(ids.shape, F32)
        for neighbour in range(fanout):
            total = total + (links_ref[neighbour : neighbour + 1, :] == ids).astype(F32)
        return total.astype(BF)

    near = counted(lax.broadcasted_iota(jnp.int32, (count, count), 0))
    copies[2].wait()
    base = jnp.where(row_text >= 0, 0.0, hist_ref[...].astype(F32))
    total = dot_t(near, base.astype(BF))
    counts_slot = dot_t(near, (row_text == slots).astype(F32).astype(BF))
    counts_text = dot_t(near, place)
    copies[3].wait()
    copies[4].wait()
    for received, source in ((received_ref[:, core], core), (across_ref[...], 1 - core)):
        received = received.reshape(size, width)
        first = received[:, 0:128].astype(F32)
        is_text = first[:, 0:1] > 24
        text = ((first[:, 0:1] - 32) * 16 + first[:, 1:2] - 32).astype(jnp.int32)
        text = jnp.where(is_text, text, -1)
        halo = received * jnp.where(is_text, 0.0, 1.0).astype(BF)
        row = lax.broadcasted_iota(jnp.int32, (size, count), 0)
        row = (row // slot_count * NC + source) * slot_count + row % slot_count
        far = counted(row + count)
        total = total + dot_t(far, halo)
        counts_slot = counts_slot + dot_t(far, (text == slots).astype(F32).astype(BF))
        counts_text = counts_text + dot_t(far, (text == text_ids).astype(F32).astype(BF))
    sum_ref[...] = total
    counts_slot_ref[...] = counts_slot.astype(BF)
    counts_text_ref[...] = counts_text.astype(BF)


def halo_sums(place, received, across, target, links, hist):
    count = hist.shape[0]
    square = jax.ShapeDtypeStruct((count, target.shape[1]), BF)
    return pl.pallas_call(
        halo_kernel,
        out_shape=(jax.ShapeDtypeStruct(hist.shape, F32), square, square),
        in_specs=scalars() + far_off(5),
        out_specs=(pl.BlockSpec(),) * 3,
        scratch_shapes=room(target, links, hist, received, across),
        name="halo_sums",
        **grant(52, 1000000000, 5000000),
    )(place, target, links, hist, received, across)


def sage_kernel(
    fanout,
    share,
    own_texts,
    place_ref,
    fresh_ref,
    other_ref,
    *refs,
):
    sources, (sage_ref, keep_ref, send_ref), targets = refs[:8], refs[8:11], refs[11:-1]
    copies = fetch(sources, targets, refs[-1])
    target_ref, counts_slot_ref, counts_text_ref, sums_ref, hist_ref = targets[:5]
    w_self_ref, w_neigh_ref, upstream_ref = targets[5:]
    half = fresh_ref.shape[0]
    quarter, width = w_self_ref.shape
    count = hist_ref.shape[0]
    texts = target_ref.shape[1]
    core, me = place_ref[CORE], place_ref[ME]
    fresh, other = fresh_ref[...], other_ref[...]

    block = share + own_texts
    wide = keep_ref.shape[0]
    ids = lax.broadcasted_iota(jnp.int32, (width + texts, wide), 0)
    column = lax.broadcasted_iota(jnp.int32, (1, wide), 1)
    stand = []
    for side in (1 - core, core):
        owner, inside = column // block * NC + side, column % block
        row = jnp.where(
            inside < share, owner * share + inside, width + owner * own_texts + inside - share
        )
        stand.append((ids == row).astype(F32).astype(BF))

    for copy in copies[:4]:
        copy.wait()
    added = dot(counts_slot_ref[:, :half], fresh) + dot(counts_slot_ref[:, half:], other)
    agg_rows = ((sums_ref[...] + added) / fanout).astype(BF)
    copies[4].wait()
    place, row_text = text_rows(target_ref[...], count, place_ref[DOM])
    place_slot = (row_text == slot_texts(texts, half // NY, core, me)).astype(F32).astype(BF)
    placed = dot(place_slot[:, :half], fresh) + dot(place_slot[:, half:], other)
    table = jnp.where(row_text >= 0, placed, hist_ref[...].astype(F32)).astype(BF)
    for copy in copies[5:]:
        copy.wait()
    pre_act = dot_nt(table, w_self_ref[...]) + dot_nt(agg_rows, w_neigh_ref[...])
    cdf = 0.5 * (1.0 + lax.erf(pre_act * math.sqrt(0.5)))
    density = jnp.exp(-0.5 * pre_act * pre_act) * (1.0 / math.sqrt(2.0 * math.pi))
    sage_ref[...] = (pre_act * cdf).T.astype(BF)
    upstream = upstream_ref[...].astype(F32).T
    grad_pre = (upstream * (cdf + pre_act * density)).astype(BF)
    self_rows = jnp.concatenate([table, place], axis=1)
    neigh_rows = jnp.concatenate([agg_rows, counts_text_ref[...]], axis=1)
    for out_ref, side in zip((send_ref, keep_ref), stand):
        out_ref[:, :quarter] = dot_t(dot(self_rows, side).astype(BF), grad_pre).astype(BF)
        out_ref[:, quarter:] = dot_t(dot(neigh_rows, side).astype(BF), grad_pre).astype(BF)


def sage(
    place, fresh, other, sums, counts, target, hist, w_self, w_neigh, upstream, fanout, share
):
    quarter, width = w_self.shape
    count, texts = hist.shape[0], target.shape[1]
    own_texts = texts * share // width
    block = jax.ShapeDtypeStruct(((width + texts) // NC, 2 * quarter), BF)
    return pl.pallas_call(
        lambda *refs: sage_kernel(fanout, share, own_texts, *refs),
        out_shape=(jax.ShapeDtypeStruct((quarter, count), BF), block, block),
        in_specs=scalars() + whole(2) + far_off(8),
        out_specs=tuple(whole(3)),
        scratch_shapes=room(target, *counts, sums, hist, w_self, w_neigh, upstream),
        name="sage",
        **grant(52, 2000000000, 8000000),
    )(place, fresh, other, target, *counts, sums, hist, w_self, w_neigh, upstream)


def combine_kernel(keep_ref, got_ref, out_ref):
    sums = keep_ref[...].astype(F32) + got_ref[...].astype(F32)
    out_ref[...] = sums.astype(BF).reshape(out_ref.shape)


def combine(keep, got, chips):
    rows, width = keep.shape
    return pl.pallas_call(
        combine_kernel,
        out_shape=jax.ShapeDtypeStruct((chips, rows // chips, width), BF),
        in_specs=whole(2),
        out_specs=whole(1)[0],
        name="combine",
        **grant(16, 200000, 1200000),
    )(keep, got)


def final_kernel(fanout, place_ref, parts_ref, w_self_hbm, w_neigh_hbm, *refs):
    self_ref, neigh_ref, term_refs = refs[0], refs[1], refs[2 : 2 + NY]
    w_self_ref, w_neigh_ref, semaphores = refs[2 + NY :]
    copies = fetch((w_self_hbm, w_neigh_hbm), (w_self_ref, w_neigh_ref), semaphores)
    share, quarter = self_ref.shape
    total = jnp.sum(parts_ref[...].astype(F32), axis=0)
    self_ref[...] = total[:share, :quarter]
    neigh_ref[...] = total[:share, quarter:]
    rows = total[share:]
    at_rows = rows[:, :quarter].astype(BF)
    at_links = (rows[:, quarter:] / fanout).astype(BF)
    for copy in copies:
        copy.wait()
    terms = dot(at_rows, w_self_ref[...]) + dot(at_links, w_neigh_ref[...])
    for s, ref in enumerate(term_refs):
        ref[...] = sliced(terms, lax.rem(place_ref[ME] + s, NY), quarter)


def final_sums(place, parts, w_self, w_neigh, share, fanout):
    quarter = w_self.shape[0]
    grads = jax.ShapeDtypeStruct((share, quarter), F32)
    texts = jax.ShapeDtypeStruct((parts.shape[1] - share, quarter), F32)
    return pl.pallas_call(
        lambda *refs: final_kernel(fanout, *refs),
        out_shape=(grads, grads) + (texts,) * NY,
        in_specs=scalars() + whole(1) + far_off(2),
        out_specs=tuple(whole(2 + NY)),
        scratch_shapes=room(w_self, w_neigh),
        name="final_sums",
        **grant(16, 10000000, 1000000),
    )(place, parts, w_self, w_neigh)


def local(
    hidden_states,
    text_len,
    w_qkv,
    w_out,
    w_up,
    w_down,
    hist,
    nbr,
    send_rows,
    fresh_target,
    w_self,
    w_neigh,
    upstream,
):
    my_x, my_z, my_c, my_y = (lax.axis_index(axis) for axis in "xzcy")
    model_width = hist.shape[1]
    peer_count, slot_count = send_rows.shape[1:]
    fanout = nbr.shape[1]
    share = model_width // peer_count
    chips = peer_count // NC
    dom = (my_x * NZ + my_z) * NC + my_c
    place = jnp.concatenate([jnp.stack([dom, my_c, my_y]).astype(jnp.int32), text_len])

    texts = (NY, hidden_states.shape[0] // NY, model_width)
    context = attend(hidden_states, text_len, w_qkv)
    attended = dot(context, w_out).astype(BF).reshape(texts)

    def part(s):
        return lax.dynamic_index_in_dim(attended, (my_y + s) % NY, 0, keepdims=False)

    residual = lax.dynamic_index_in_dim(hidden_states.reshape(texts), my_y, 0, keepdims=False)
    parts = [part(0)] + [pull(part(NY - s), "y", s) for s in (2, 1, 3)]
    first_norm = first_layer_norm(residual, parts)

    target = fresh_target[None, :]
    attended, wanted = lax.optimization_barrier((attended, send_rows))
    wanted = wanted.reshape(peer_count * slot_count, 1)
    outgoing = outgoing_rows(place, target, wanted, hist, chips)
    received = lax.all_to_all(outgoing, ("x", "z"), split_axis=0, concat_axis=0, tiled=True)

    others = {s: pull(first_norm, "y", s) for s in (1, 3, 2)}
    own, up, down = feed_first(first_norm, w_up, w_down)
    parts = [own] + [pull(feed(others[s], up, down), "y", NY - s) for s in (1, 3, 2)]
    fresh_row = pooled_row(place, first_norm, parts)

    rows = spread_rows([fresh_row] + [pull(fresh_row, "y", s) for s in (1, 3, 2)], chips)
    _, received = lax.optimization_barrier((rows, received))
    fresh = lax.all_to_all(rows, ("x", "z"), split_axis=0, concat_axis=0, tiled=True)
    across = pull(lax.dynamic_index_in_dim(received, 1 - my_c, 1, keepdims=False), "c", 1)
    sums, *counts = halo_sums(place, received, across, target, nbr.T, hist)
    fresh, sums = lax.optimization_barrier((fresh, sums))
    fresh = fresh.reshape(-1, model_width)
    other = pull(fresh, "c", 1)

    sage_out, keep, send = sage(
        place,
        fresh,
        other,
        sums,
        counts,
        target,
        hist,
        w_self.T,
        w_neigh.T,
        upstream.T,
        fanout,
        share,
    )
    parts = combine(keep, pull(send, "c", 1), chips)
    parts = lax.all_to_all(parts, ("x", "z"), split_axis=0, concat_axis=0, tiled=True)
    grad_self_w, grad_neigh_w, grad_fresh, *terms = final_sums(
        place, parts, w_self.T, w_neigh.T, share, fanout
    )
    for s in (2, 1, 3):
        grad_fresh = grad_fresh + pull(terms[NY - s - 1], "y", s)
    return (sage_out.T, grad_fresh, grad_self_w, grad_neigh_w)


def solution(mesh):
    dom = ("x", "z", "c")
    split = Mesh(mesh.devices.reshape(NX, NZ, NC, NY), dom + ("y",))
    in_specs = (
        P(dom, None),
        P(dom),
        P(None, None, "y"),
        P("y", None),
        P(None, "y"),
        P("y", None),
        P(dom, None),
        P(dom, None),
        P(dom, None, None),
        P(),
        P(None, "y"),
        P(None, "y"),
        P(dom, "y"),
    )
    out_specs = (P(dom, "y"),) * 4
    return jax.shard_map(local, mesh=split, in_specs=in_specs, out_specs=out_specs, check_vma=False)
```

```python
import math

import jax
import jax.numpy as jnp
from jax import lax
from jax.experimental import pallas as pl
from jax.experimental.pallas import tpu as pltpu
from jax.sharding import Mesh, PartitionSpec as P

HEADS = 12
EPSILON = 1e-05
NX, NZ, NC, NY = 4, 8, 2, 4
BF = jnp.bfloat16
F32 = jnp.float32


def layer_norm(values):
    center = values - jnp.mean(values, axis=-1, keepdims=True)
    spread = jnp.mean(center * center, axis=-1, keepdims=True)
    return center * lax.rsqrt(spread + EPSILON)


def exact_gelu(values):
    return 0.5 * values * (1.0 + lax.erf(values * math.sqrt(0.5)))


def dot(a, b):
    return jnp.dot(a, b, preferred_element_type=F32)


def dot_t(a, b):
    return lax.dot_general(a, b, (((0,), (0,)), ((), ())), preferred_element_type=F32)


def dot_nt(a, b):
    return lax.dot_general(a, b, (((1,), (1,)), ((), ())), preferred_element_type=F32)


def pull(value, axis, shift):
    count = {"x": NX, "z": NZ, "c": NC, "y": NY}[axis]
    return lax.ppermute(value, axis, [((i + shift) % count, i) for i in range(count)])


def whole(count):
    return [pl.BlockSpec(memory_space=pltpu.VMEM)] * count


def far_off(count):
    return [pl.BlockSpec(memory_space=pltpu.HBM)] * count


def scalars():
    return [pl.BlockSpec(memory_space=pltpu.SMEM)]


def grant(mib, flops, bytes_accessed):
    return {
        "compiler_params": pltpu.CompilerParams(vmem_limit_bytes=mib * 2**20),
        "cost_estimate": pl.CostEstimate(
            flops=flops, bytes_accessed=bytes_accessed, transcendentals=0
        ),
    }


def room(*arrays):
    return [pltpu.VMEM(a.shape, a.dtype) for a in arrays] + [pltpu.SemaphoreType.DMA((len(arrays),))]


def fetch(sources, targets, semaphores):
    copies = [
        pltpu.make_async_copy(source, target, semaphores.at[k])
        for k, (source, target) in enumerate(zip(sources, targets))
    ]
    for copy in copies:
        copy.start()
    return copies


DOM, CORE, ME, LENGTHS = 0, 1, 2, 3


def attend(rows, lengths, weights_qkv):
    model_width = rows.shape[1]
    text_count = lengths.shape[0]
    length = rows.shape[0] // text_count
    local_width = weights_qkv.shape[2]
    head_dim = model_width // HEADS
    head_count = local_width // head_dim
    packed = dot(rows, weights_qkv.reshape(model_width, 3 * local_width)).astype(BF)
    packed = packed.reshape(text_count, length, 3, head_count, head_dim)
    scores = jnp.einsum(
        "tqhc,tkhc->thqk", packed[:, :, 0], packed[:, :, 1], preferred_element_type=F32
    ) / math.sqrt(head_dim)
    live_keys = jnp.arange(length)[None, :] < lengths[:, None]
    scores = jnp.where(live_keys[:, None, None, :], scores, -1e30)
    row_peak = jnp.max(scores, axis=-1, keepdims=True)
    weights = jnp.exp(scores - row_peak)
    attention_probs = (weights / jnp.sum(weights, axis=-1, keepdims=True)).astype(BF)
    context = jnp.einsum(
        "thqk,tkhc->tqhc", attention_probs, packed[:, :, 2], preferred_element_type=F32
    )
    return context.astype(BF).reshape(text_count * length, local_width)


def norm_kernel(residual_ref, own_ref, near_ref, far_ref, across_ref, out_ref):
    total = residual_ref[...].astype(F32) + own_ref[...].astype(F32)
    for ref in (near_ref, far_ref, across_ref):
        total = total + ref[...].astype(F32)
    out_ref[...] = layer_norm(total).astype(BF)


def first_layer_norm(residual, parts):
    return pl.pallas_call(
        norm_kernel,
        out_shape=jax.ShapeDtypeStruct(residual.shape, BF),
        in_specs=whole(5),
        out_specs=whole(1)[0],
        name="first_norm",
        **grant(16, 4000000000, 1200000),
    )(residual, *parts)


def feed_kernel(block_ref, up_ref, down_ref, out_ref):
    inner = exact_gelu(dot(block_ref[...], up_ref[...])).astype(BF)
    out_ref[...] = dot(inner, down_ref[...]).astype(out_ref.dtype)


def feed_first_kernel(block_ref, up_hbm, down_hbm, out_ref, up_ref, down_ref, semaphores):
    copies = fetch((up_hbm, down_hbm), (up_ref, down_ref), semaphores)
    copies[0].wait()
    inner = exact_gelu(dot(block_ref[...], up_ref[...])).astype(BF)
    copies[1].wait()
    out_ref[...] = dot(inner, down_ref[...])


def feed_first(block, w_up, w_down):
    return pl.pallas_call(
        feed_first_kernel,
        out_shape=(
            jax.ShapeDtypeStruct(block.shape, F32),
            jax.ShapeDtypeStruct(w_up.shape, BF),
            jax.ShapeDtypeStruct(w_down.shape, BF),
        ),
        in_specs=whole(1) + far_off(2),
        out_specs=tuple(whole(3)),
        scratch_shapes=[pltpu.SemaphoreType.DMA((2,))],
        name="feed_first",
        **grant(16, 8000000000, 9000000),
    )(block, w_up, w_down)


def feed(block, w_up, w_down):
    return pl.pallas_call(
        feed_kernel,
        out_shape=jax.ShapeDtypeStruct(block.shape, BF),
        in_specs=whole(3),
        out_specs=whole(1)[0],
        name="feed",
        **grant(16, 8000000000, 9000000),
    )(block, w_up, w_down)


def pool_kernel(place_ref, first_ref, own_ref, near_ref, far_ref, across_ref, out_ref):
    total = first_ref[...].astype(F32) + own_ref[...]
    for ref in (near_ref, far_ref, across_ref):
        total = total + ref[...].astype(F32)
    normed = layer_norm(total)
    length = place_ref[LENGTHS + place_ref[ME]]
    live = lax.broadcasted_iota(jnp.int32, normed.shape, 0) < length
    pooled = jnp.sum(jnp.where(live, normed, 0.0), axis=0, keepdims=True)
    out_ref[...] = (pooled / length.astype(F32)).astype(BF)


def pooled_row(place, first_norm, parts):
    return pl.pallas_call(
        pool_kernel,
        out_shape=jax.ShapeDtypeStruct((1, first_norm.shape[1]), BF),
        in_specs=scalars() + whole(5),
        out_specs=whole(1)[0],
        name="pooled_row",
        **grant(16, 4000000000, 1200000),
    )(place, first_norm, *parts)


def spread_kernel(own_ref, near_ref, far_ref, across_ref, out_ref):
    refs = (own_ref, near_ref, far_ref, across_ref)
    index = lax.broadcasted_iota(jnp.int32, out_ref.shape[1:], 0)
    rows = jnp.zeros(out_ref.shape[1:], F32)
    for s, ref in enumerate(refs):
        rows = jnp.where(index == s, ref[...].astype(F32), rows)
    out_ref[...] = jnp.broadcast_to(rows.astype(BF)[None], out_ref.shape)


def spread_rows(rows, chips):
    return pl.pallas_call(
        spread_kernel,
        out_shape=jax.ShapeDtypeStruct((chips, len(rows), rows[0].shape[1]), BF),
        in_specs=whole(len(rows)),
        out_specs=whole(1)[0],
        name="spread_rows",
        **grant(16, 1000000, 200000),
    )(*rows)


def sliced(values, index, width):
    total = values[:, :width]
    for k in range(1, values.shape[1] // width):
        total = jnp.where(index == k, values[:, k * width : (k + 1) * width], total)
    return total


def text_rows(target, count, dom):
    shape = (count, target.shape[1])
    row_ids = lax.broadcasted_iota(jnp.int32, shape, 0) + dom * count
    text_ids = lax.broadcasted_iota(jnp.int32, shape, 1)
    holds = row_ids == target
    row_text = jnp.sum(jnp.where(holds, text_ids + 1, 0), axis=1, keepdims=True) - 1
    return holds.astype(F32).astype(BF), row_text


def slot_texts(texts, chips, core, me):
    slot = lax.broadcasted_iota(jnp.int32, (1, texts), 1)
    step = slot % NY
    slot_y = ((step ^ (step >> 1)) + me) % NY
    slot_core = (slot // (chips * NY) + core) % NC
    return ((slot // NY % chips) * NC + slot_core) * NY + slot_y


def outgoing_kernel(place_ref, target_ref, wanted_ref, hist_hbm, out_ref, hist_ref, semaphores):
    copies = fetch((hist_hbm,), (hist_ref,), semaphores)
    count, width = hist_ref.shape
    _, row_text = text_rows(target_ref[...], count, place_ref[DOM])
    column = lax.broadcasted_iota(jnp.int32, (count, width), 1)
    code = jnp.where(
        column == 0, 32 + row_text // 16, jnp.where(column == 1, 32 + row_text % 16, 0)
    ).astype(F32)
    ids = lax.broadcasted_iota(jnp.int32, (wanted_ref.shape[0], count), 1)
    pick = (wanted_ref[...] == ids).astype(F32).astype(BF)
    copies[0].wait()
    coded = jnp.where(row_text >= 0, code, hist_ref[...].astype(F32)).astype(BF)
    out_ref[...] = dot(pick, coded).astype(BF).reshape(out_ref.shape)


def outgoing_rows(place, target, wanted, hist, chips):
    rows, width = wanted.shape[0], hist.shape[1]
    return pl.pallas_call(
        outgoing_kernel,
        out_shape=jax.ShapeDtypeStruct((chips, NC, rows // chips // NC, width), BF),
        in_specs=scalars() + whole(2) + far_off(1),
        out_specs=pl.BlockSpec(),
        scratch_shapes=room(hist),
        name="outgoing_rows",
        **grant(52, 2000000000, 6000000),
    )(place, target, wanted, hist)


def halo_kernel(
    place_ref,
    target_hbm,
    links_hbm,
    hist_hbm,
    received_hbm,
    across_hbm,
    sum_ref,
    counts_slot_ref,
    counts_text_ref,
    target_ref,
    links_ref,
    hist_ref,
    received_ref,
    across_ref,
    semaphores,
):
    copies = fetch(
        (target_hbm, links_hbm, hist_hbm, received_hbm, across_hbm),
        (target_ref, links_ref, hist_ref, received_ref, across_ref),
        semaphores,
    )
    chips, slot_count, width = across_ref.shape
    size = chips * slot_count
    fanout, count = links_ref.shape
    texts = target_ref.shape[1]
    core, me = place_ref[CORE], place_ref[ME]
    slots = slot_texts(texts, chips, core, me)
    text_ids = lax.broadcasted_iota(jnp.int32, slots.shape, 1)
    copies[0].wait()
    copies[1].wait()
    place, row_text = text_rows(target_ref[...], count, place_ref[DOM])

    def counted(ids):
        total = jnp.zeros(ids.shape, F32)
        for neighbour in range(fanout):
            total = total + (links_ref[neighbour : neighbour + 1, :] == ids).astype(F32)
        return total.astype(BF)

    near = counted(lax.broadcasted_iota(jnp.int32, (count, count), 0))
    copies[2].wait()
    base = jnp.where(row_text >= 0, 0.0, hist_ref[...].astype(F32))
    total = dot_t(near, base.astype(BF))
    counts_slot = dot_t(near, (row_text == slots).astype(F32).astype(BF))
    counts_text = dot_t(near, place)
    copies[3].wait()
    copies[4].wait()
    for received, source in ((received_ref[:, core], core), (across_ref[...], 1 - core)):
        received = received.reshape(size, width)
        first = received[:, 0:128].astype(F32)
        is_text = first[:, 0:1] > 24
        text = ((first[:, 0:1] - 32) * 16 + first[:, 1:2] - 32).astype(jnp.int32)
        text = jnp.where(is_text, text, -1)
        halo = received * jnp.where(is_text, 0.0, 1.0).astype(BF)
        row = lax.broadcasted_iota(jnp.int32, (size, count), 0)
        row = (row // slot_count * NC + source) * slot_count + row % slot_count
        far = counted(row + count)
        total = total + dot_t(far, halo)
        counts_slot = counts_slot + dot_t(far, (text == slots).astype(F32).astype(BF))
        counts_text = counts_text + dot_t(far, (text == text_ids).astype(F32).astype(BF))
    sum_ref[...] = total
    counts_slot_ref[...] = counts_slot.astype(BF)
    counts_text_ref[...] = counts_text.astype(BF)


def halo_sums(place, received, across, target, links, hist):
    count = hist.shape[0]
    square = jax.ShapeDtypeStruct((count, target.shape[1]), BF)
    return pl.pallas_call(
        halo_kernel,
        out_shape=(jax.ShapeDtypeStruct(hist.shape, F32), square, square),
        in_specs=scalars() + far_off(5),
        out_specs=(pl.BlockSpec(),) * 3,
        scratch_shapes=room(target, links, hist, received, across),
        name="halo_sums",
        **grant(52, 1000000000, 5000000),
    )(place, target, links, hist, received, across)


def head_kernel(fanout, place_ref, fresh_ref, *refs):
    sources, semaphores, (counts_ref, sums_ref, hist_ref, target_ref, up_ref) = (
        refs[:8],
        refs[-6],
        refs[-5:],
    )
    table_ref, agg_ref, other_ref, texts_ref, w_self_ref, w_neigh_ref, upstream_ref = refs[8:-6]
    target_hbm, counts_hbm, texts_hbm, sums_hbm, hist_hbm, w_self_hbm, w_neigh_hbm, up_hbm = sources
    copies = fetch(
        (counts_hbm, sums_hbm, target_hbm, hist_hbm, up_hbm, texts_hbm, w_self_hbm, w_neigh_hbm),
        (
            counts_ref,
            sums_ref,
            target_ref,
            hist_ref,
            up_ref,
            texts_ref.at[1],
            w_self_ref,
            w_neigh_ref,
        ),
        semaphores,
    )
    half = fresh_ref.shape[0]
    count = hist_ref.shape[0]
    fresh = fresh_ref[...]
    copies[0].wait()
    copies[1].wait()
    agg_ref[...] = sums_ref[...] + dot(counts_ref[:, :half], fresh)
    other_ref[1] = counts_ref[:, half:]
    copies[2].wait()
    place, row_text = text_rows(target_ref[...], count, place_ref[DOM])
    texts_ref[0] = place
    slots = slot_texts(place.shape[1], half // NY, place_ref[CORE], place_ref[ME])
    place_slot = (row_text == slots).astype(F32).astype(BF)
    other_ref[0] = place_slot[:, half:]
    placed = dot(place_slot[:, :half], fresh)
    copies[3].wait()
    table_ref[...] = jnp.where(row_text >= 0, placed, hist_ref[...].astype(F32)).astype(BF)
    copies[4].wait()
    upstream_ref[...] = up_ref[...].astype(F32).T
    for copy in copies[5:]:
        copy.wait()


def sage_head(place, fresh, counts, sums, target, hist, w_self, w_neigh, upstream, fanout):
    counts_slot, counts_text = counts
    count, texts = counts_text.shape
    return pl.pallas_call(
        lambda *refs: head_kernel(fanout, *refs),
        out_shape=(
            jax.ShapeDtypeStruct(hist.shape, BF),
            jax.ShapeDtypeStruct(hist.shape, F32),
            jax.ShapeDtypeStruct((2, count, texts - fresh.shape[0]), BF),
            jax.ShapeDtypeStruct((2, count, texts), BF),
            jax.ShapeDtypeStruct(w_self.shape, BF),
            jax.ShapeDtypeStruct(w_neigh.shape, BF),
            jax.ShapeDtypeStruct(upstream.shape[::-1], F32),
        ),
        in_specs=scalars() + whole(1) + far_off(8),
        out_specs=tuple(whole(7)),
        scratch_shapes=[
            pltpu.SemaphoreType.DMA((8,)),
            pltpu.VMEM(counts_slot.shape, BF),
            pltpu.VMEM(sums.shape, F32),
            pltpu.VMEM(hist.shape, BF),
            pltpu.VMEM(target.shape, jnp.int32),
            pltpu.VMEM(upstream.shape, BF),
        ],
        name="sage_head",
        **grant(48, 3000000000, 4000000),
    )(place, fresh, target, counts_slot, counts_text, sums, hist, w_self, w_neigh, upstream)


def sage_kernel(
    fanout,
    place_ref,
    fresh_ref,
    table_ref,
    agg_ref,
    other_ref,
    texts_ref,
    w_self_ref,
    w_neigh_ref,
    upstream_ref,
    act_ref,
    weights_ref,
    terms_ref,
    send_ref,
    blocks_ref,
):
    fresh = fresh_ref[...]
    quarter = w_self_ref.shape[0]
    table = table_ref[...] + dot(other_ref[0], fresh).astype(BF)
    agg_rows = ((agg_ref[...] + dot(other_ref[1], fresh)) / fanout).astype(BF)
    pre_act = dot_nt(table, w_self_ref[...]) + dot_nt(agg_rows, w_neigh_ref[...])
    cdf = 0.5 * (1.0 + lax.erf(pre_act * math.sqrt(0.5)))
    density = jnp.exp(-0.5 * pre_act * pre_act) * (1.0 / math.sqrt(2.0 * math.pi))
    act_ref[...] = pre_act * cdf
    grad_pre = (upstream_ref[...] * (cdf + pre_act * density)).astype(BF)
    chips = weights_ref.shape[0]
    for k, rows in enumerate((table, agg_rows)):
        part = slice(k * quarter, (k + 1) * quarter)
        weights_ref[:, :, part] = dot_t(rows, grad_pre).reshape(chips, -1, quarter)
        terms_ref[:, :, part] = dot_t(texts_ref[k], grad_pre).reshape(chips, -1, quarter)
    put_blocks(1 - place_ref[CORE], weights_ref, terms_ref, blocks_ref)
    send_ref[...] = blocks_ref[...].astype(BF)


def put_blocks(side, weights_ref, terms_ref, blocks_ref):
    share, own_texts = weights_ref.shape[1] // NC, terms_ref.shape[1] // NC
    for core in range(NC):

        @pl.when(side == core)
        def _():
            rows = slice(core * share, (core + 1) * share)
            blocks_ref[:, :share, :] = weights_ref[:, rows, :]
            rows = slice(core * own_texts, (core + 1) * own_texts)
            blocks_ref[:, share:, :] = terms_ref[:, rows, :]


def sage(place, fresh, table, agg, other, texts, w_self, w_neigh, upstream, fanout, chips):
    quarter, width = w_self.shape
    count = table.shape[0]
    share, own_texts = width // chips, texts.shape[2] // chips
    block = (chips, (share + own_texts) // NC, 2 * quarter)
    return pl.pallas_call(
        lambda *refs: sage_kernel(fanout, *refs),
        out_shape=(
            jax.ShapeDtypeStruct((count, quarter), F32),
            jax.ShapeDtypeStruct((chips, share, 2 * quarter), F32),
            jax.ShapeDtypeStruct((chips, own_texts, 2 * quarter), F32),
            jax.ShapeDtypeStruct(block, BF),
        ),
        in_specs=scalars() + whole(8),
        out_specs=tuple(whole(4)),
        scratch_shapes=[pltpu.VMEM(block, F32)],
        name="sage",
        **grant(16, 2000000000, 8000000),
    )(place, fresh, table, agg, other, texts, w_self, w_neigh, upstream)


def tail_kernel(place_ref, act_ref, weights_ref, terms_ref, sage_ref, keep_ref):
    sage_ref[...] = act_ref[...].T.astype(BF)
    put_blocks(place_ref[CORE], weights_ref, terms_ref, keep_ref)


def sage_tail(place, act, weights, terms, send):
    return pl.pallas_call(
        tail_kernel,
        out_shape=(
            jax.ShapeDtypeStruct(act.shape[::-1], BF),
            jax.ShapeDtypeStruct(send.shape, F32),
        ),
        in_specs=scalars() + whole(3),
        out_specs=tuple(whole(2)),
        name="sage_tail",
        **grant(16, 3000000000, 4000000),
    )(place, act, weights, terms)


def combine_kernel(keep_ref, got_ref, out_ref):
    sums = keep_ref[...] + got_ref[...].astype(F32)
    out_ref[...] = sums.astype(BF)


def combine(keep, got):
    return pl.pallas_call(
        combine_kernel,
        out_shape=jax.ShapeDtypeStruct(got.shape, BF),
        in_specs=whole(2),
        out_specs=whole(1)[0],
        name="combine",
        **grant(16, 200000, 1200000),
    )(keep, got)


def final_kernel(
    fanout, place_ref, parts_ref, w_self_ref, w_neigh_ref, self_ref, neigh_ref, *term_refs
):
    share, quarter = self_ref.shape
    total = jnp.sum(parts_ref[...].astype(F32), axis=0)
    self_ref[...] = total[:share, :quarter]
    neigh_ref[...] = total[:share, quarter:]
    rows = total[share:]
    at_rows = rows[:, :quarter].astype(BF)
    at_links = (rows[:, quarter:] / fanout).astype(BF)
    terms = dot(at_rows, w_self_ref[...]) + dot(at_links, w_neigh_ref[...])
    for s, ref in enumerate(term_refs):
        ref[...] = sliced(terms, lax.rem(place_ref[ME] + s, NY), quarter)


def final_sums(place, parts, w_self, w_neigh, share, fanout):
    quarter = w_self.shape[0]
    grads = jax.ShapeDtypeStruct((share, quarter), F32)
    texts = jax.ShapeDtypeStruct((parts.shape[1] - share, quarter), F32)
    return pl.pallas_call(
        lambda *refs: final_kernel(fanout, *refs),
        out_shape=(grads, grads) + (texts,) * NY,
        in_specs=scalars() + whole(3),
        out_specs=tuple(whole(2 + NY)),
        name="final_sums",
        **grant(16, 10000000, 1000000),
    )(place, parts, w_self, w_neigh)


def local(
    hidden_states,
    text_len,
    w_qkv,
    w_out,
    w_up,
    w_down,
    hist,
    nbr,
    send_rows,
    fresh_target,
    w_self,
    w_neigh,
    upstream,
):
    my_x, my_z, my_c, my_y = (lax.axis_index(axis) for axis in "xzcy")
    model_width = hist.shape[1]
    peer_count, slot_count = send_rows.shape[1:]
    fanout = nbr.shape[1]
    share = model_width // peer_count
    chips = peer_count // NC
    dom = (my_x * NZ + my_z) * NC + my_c

    texts = (NY, hidden_states.shape[0] // NY, model_width)
    context = attend(hidden_states, text_len, w_qkv)
    attended = dot(context, w_out).astype(BF).reshape(texts)

    def part(s):
        return lax.dynamic_index_in_dim(attended, (my_y + s) % NY, 0, keepdims=False)

    residual = lax.dynamic_index_in_dim(hidden_states.reshape(texts), my_y, 0, keepdims=False)
    parts = [part(0)] + [pull(part(NY - s), "y", s) for s in (2, 1, 3)]
    first_norm = first_layer_norm(residual, parts)

    target = fresh_target[None, :]
    attended, wanted, lengths = lax.optimization_barrier((attended, send_rows, text_len))
    place = jnp.concatenate([jnp.stack([dom, my_c, my_y]).astype(jnp.int32), lengths])
    wanted = wanted.reshape(peer_count * slot_count, 1)
    outgoing = outgoing_rows(place, target, wanted, hist, chips)
    received = lax.all_to_all(outgoing, ("x", "z"), split_axis=0, concat_axis=0, tiled=True)

    others = {s: pull(first_norm, "y", s) for s in (1, 3, 2)}
    own, up, down = feed_first(first_norm, w_up, w_down)
    parts = [own] + [pull(feed(others[s], up, down), "y", NY - s) for s in (1, 3, 2)]
    fresh_row = pooled_row(place, first_norm, parts)

    rows = spread_rows([fresh_row] + [pull(fresh_row, "y", s) for s in (1, 3, 2)], chips)
    _, received = lax.optimization_barrier((rows, received))
    fresh = lax.all_to_all(rows, ("x", "z"), split_axis=0, concat_axis=0, tiled=True)
    across = pull(lax.dynamic_index_in_dim(received, 1 - my_c, 1, keepdims=False), "c", 1)
    sums, *counts = halo_sums(place, received, across, target, nbr.T, hist)
    fresh, sums = lax.optimization_barrier((fresh, sums))
    fresh = fresh.reshape(-1, model_width)
    other = pull(fresh, "c", 1)

    begun = sage_head(
        place, fresh, counts, sums, target, hist, w_self.T, w_neigh.T, upstream.T, fanout
    )
    act, weights, terms, send = sage(place, other, *begun, fanout, chips)
    sage_out, keep = sage_tail(place, act, weights, terms, send)
    parts = combine(keep, pull(send, "c", 1))
    parts = lax.all_to_all(parts, ("x", "z"), split_axis=0, concat_axis=0, tiled=True)
    grad_self_w, grad_neigh_w, grad_fresh, *terms = final_sums(
        place, parts, w_self.T, w_neigh.T, share, fanout
    )
    for s in (2, 1, 3):
        grad_fresh = grad_fresh + pull(terms[NY - s - 1], "y", s)
    return (sage_out.T, grad_fresh, grad_self_w, grad_neigh_w)


def solution(mesh):
    dom = ("x", "z", "c")
    split = Mesh(mesh.devices.reshape(NX, NZ, NC, NY), dom + ("y",))
    in_specs = (
        P(dom, None),
        P(dom),
        P(None, None, "y"),
        P("y", None),
        P(None, "y"),
        P("y", None),
        P(dom, None),
        P(dom, None),
        P(dom, None, None),
        P(),
        P(None, "y"),
        P(None, "y"),
        P(dom, "y"),
    )
    out_specs = (P(dom, "y"),) * 4
    return jax.shard_map(local, mesh=split, in_specs=in_specs, out_specs=out_specs, check_vma=False)
```

```python
import math

import jax
import jax.numpy as jnp
from jax import lax
from jax.experimental import pallas as pl
from jax.experimental.pallas import tpu as pltpu
from jax.sharding import Mesh, PartitionSpec as P

HEADS = 12
EPSILON = 1e-05
NX, NZ, NC, NY = 4, 8, 2, 4
BF = jnp.bfloat16
F32 = jnp.float32


def layer_norm(values):
    center = values - jnp.mean(values, axis=-1, keepdims=True)
    spread = jnp.mean(center * center, axis=-1, keepdims=True)
    return center * lax.rsqrt(spread + EPSILON)


def exact_gelu(values):
    return 0.5 * values * (1.0 + lax.erf(values * math.sqrt(0.5)))


def dot(a, b):
    return jnp.dot(a, b, preferred_element_type=F32)


def dot_t(a, b):
    return lax.dot_general(a, b, (((0,), (0,)), ((), ())), preferred_element_type=F32)


def dot_nt(a, b):
    return lax.dot_general(a, b, (((1,), (1,)), ((), ())), preferred_element_type=F32)


def swap(value):
    return lax.ppermute(value, "y", [(i, i ^ 1) for i in range(NY)])


def pull(value, axis, shift):
    count = {"x": NX, "z": NZ, "c": NC, "y": NY}[axis]
    return lax.ppermute(value, axis, [((i + shift) % count, i) for i in range(count)])


def whole(count):
    return [pl.BlockSpec(memory_space=pltpu.VMEM)] * count


def far_off(count):
    return [pl.BlockSpec(memory_space=pltpu.HBM)] * count


def scalars():
    return [pl.BlockSpec(memory_space=pltpu.SMEM)]


def grant(mib, flops, bytes_accessed):
    return {
        "compiler_params": pltpu.CompilerParams(vmem_limit_bytes=mib * 2**20),
        "cost_estimate": pl.CostEstimate(
            flops=flops, bytes_accessed=bytes_accessed, transcendentals=0
        ),
    }


def room(*arrays):
    return [pltpu.VMEM(a.shape, a.dtype) for a in arrays] + [pltpu.SemaphoreType.DMA((len(arrays),))]


def fetch(sources, targets, semaphores):
    copies = [
        pltpu.make_async_copy(source, target, semaphores.at[k])
        for k, (source, target) in enumerate(zip(sources, targets))
    ]
    for copy in copies:
        copy.start()
    return copies


DOM, CORE, ME, LENGTHS = 0, 1, 2, 3


def attend(rows, lengths, weights_qkv):
    model_width = rows.shape[1]
    text_count = lengths.shape[0]
    length = rows.shape[0] // text_count
    local_width = weights_qkv.shape[2]
    head_dim = model_width // HEADS
    head_count = local_width // head_dim
    packed = dot(rows, weights_qkv.reshape(model_width, 3 * local_width)).astype(BF)
    packed = packed.reshape(text_count, length, 3, head_count, head_dim)
    scores = jnp.einsum(
        "tqhc,tkhc->thqk", packed[:, :, 0], packed[:, :, 1], preferred_element_type=F32
    ) / math.sqrt(head_dim)
    live_keys = jnp.arange(length)[None, :] < lengths[:, None]
    scores = jnp.where(live_keys[:, None, None, :], scores, -1e30)
    row_peak = jnp.max(scores, axis=-1, keepdims=True)
    weights = jnp.exp(scores - row_peak)
    attention_probs = (weights / jnp.sum(weights, axis=-1, keepdims=True)).astype(BF)
    context = jnp.einsum(
        "thqk,tkhc->tqhc", attention_probs, packed[:, :, 2], preferred_element_type=F32
    )
    return context.astype(BF).reshape(text_count * length, local_width)


def norm_kernel(residual_ref, own_ref, near_ref, far_ref, across_ref, out_ref):
    total = residual_ref[...].astype(F32) + own_ref[...].astype(F32)
    for ref in (near_ref, far_ref, across_ref):
        total = total + ref[...].astype(F32)
    out_ref[...] = layer_norm(total).astype(BF)


def first_layer_norm(residual, parts):
    return pl.pallas_call(
        norm_kernel,
        out_shape=jax.ShapeDtypeStruct(residual.shape, BF),
        in_specs=whole(5),
        out_specs=whole(1)[0],
        name="first_norm",
        **grant(16, 4000000000, 1200000),
    )(residual, *parts)


def feed_kernel(block_ref, up_ref, down_ref, out_ref):
    inner = exact_gelu(dot(block_ref[...], up_ref[...])).astype(BF)
    out_ref[...] = dot(inner, down_ref[...]).astype(out_ref.dtype)


def feed_first_kernel(block_ref, up_hbm, down_hbm, out_ref, up_ref, down_ref, semaphores):
    copies = fetch((up_hbm, down_hbm), (up_ref, down_ref), semaphores)
    copies[0].wait()
    inner = exact_gelu(dot(block_ref[...], up_ref[...])).astype(BF)
    copies[1].wait()
    out_ref[...] = dot(inner, down_ref[...])


def feed_first(block, w_up, w_down):
    return pl.pallas_call(
        feed_first_kernel,
        out_shape=(
            jax.ShapeDtypeStruct(block.shape, F32),
            jax.ShapeDtypeStruct(w_up.shape, BF),
            jax.ShapeDtypeStruct(w_down.shape, BF),
        ),
        in_specs=whole(1) + far_off(2),
        out_specs=tuple(whole(3)),
        scratch_shapes=[pltpu.SemaphoreType.DMA((2,))],
        name="feed_first",
        **grant(16, 8000000000, 9000000),
    )(block, w_up, w_down)


def feed(block, w_up, w_down):
    return pl.pallas_call(
        feed_kernel,
        out_shape=jax.ShapeDtypeStruct(block.shape, BF),
        in_specs=whole(3),
        out_specs=whole(1)[0],
        name="feed",
        **grant(16, 8000000000, 9000000),
    )(block, w_up, w_down)


def pool_kernel(place_ref, first_ref, own_ref, near_ref, far_ref, across_ref, out_ref):
    total = first_ref[...].astype(F32) + own_ref[...]
    for ref in (near_ref, far_ref, across_ref):
        total = total + ref[...].astype(F32)
    normed = layer_norm(total)
    length = place_ref[LENGTHS + place_ref[ME]]
    live = lax.broadcasted_iota(jnp.int32, normed.shape, 0) < length
    pooled = jnp.sum(jnp.where(live, normed, 0.0), axis=0, keepdims=True)
    out_ref[...] = (pooled / length.astype(F32)).astype(BF)


def pooled_row(place, first_norm, parts):
    return pl.pallas_call(
        pool_kernel,
        out_shape=jax.ShapeDtypeStruct((1, first_norm.shape[1]), BF),
        in_specs=scalars() + whole(5),
        out_specs=whole(1)[0],
        name="pooled_row",
        **grant(16, 4000000000, 1200000),
    )(place, first_norm, *parts)


def spread_kernel(own_ref, near_ref, far_ref, across_ref, out_ref):
    refs = (own_ref, near_ref, far_ref, across_ref)
    index = lax.broadcasted_iota(jnp.int32, out_ref.shape[1:], 0)
    rows = jnp.zeros(out_ref.shape[1:], F32)
    for s, ref in enumerate(refs):
        rows = jnp.where(index == s, ref[...].astype(F32), rows)
    out_ref[...] = jnp.broadcast_to(rows.astype(BF)[None], out_ref.shape)


def spread_rows(rows, chips):
    return pl.pallas_call(
        spread_kernel,
        out_shape=jax.ShapeDtypeStruct((chips, len(rows), rows[0].shape[1]), BF),
        in_specs=whole(len(rows)),
        out_specs=whole(1)[0],
        name="spread_rows",
        **grant(16, 1000000, 200000),
    )(*rows)


def sliced(values, index, width):
    total = values[:, :width]
    for k in range(1, values.shape[1] // width):
        total = jnp.where(index == k, values[:, k * width : (k + 1) * width], total)
    return total


def text_rows(target, count, dom):
    shape = (count, target.shape[1])
    row_ids = lax.broadcasted_iota(jnp.int32, shape, 0) + dom * count
    text_ids = lax.broadcasted_iota(jnp.int32, shape, 1)
    holds = row_ids == target
    row_text = jnp.sum(jnp.where(holds, text_ids + 1, 0), axis=1, keepdims=True) - 1
    return holds.astype(F32).astype(BF), row_text


def slot_texts(texts, chips, core, me):
    slot = lax.broadcasted_iota(jnp.int32, (1, texts), 1)
    step = slot % NY
    slot_y = ((step ^ (step >> 1)) + me) % NY
    slot_core = (slot // (chips * NY) + core) % NC
    return ((slot // NY % chips) * NC + slot_core) * NY + slot_y


def outgoing_kernel(
    place_ref, target_ref, wanted_ref, hist_hbm, out_hbm, hist_ref, semaphores, rows_ref, out_sems
):
    copies = fetch((hist_hbm,), (hist_ref,), semaphores)
    count, width = hist_ref.shape[0], rows_ref.shape[3]
    _, row_text = text_rows(target_ref[...], count, place_ref[DOM])
    column = lax.broadcasted_iota(jnp.int32, (count, width), 1)
    code = jnp.where(
        column == 0, 32 + row_text // 16, jnp.where(column == 1, 32 + row_text % 16, 0)
    ).astype(F32)
    parts = out_sems.shape[0]
    chips = rows_ref.shape[0] // parts
    size = wanted_ref.shape[0] // parts
    ids = lax.broadcasted_iota(jnp.int32, (size, count), 1)
    copies[0].wait()
    hist = sliced(hist_ref[...].astype(F32), place_ref[ME] % 2, width)
    coded = jnp.where(row_text >= 0, code, hist).astype(BF)
    sent = []
    for part in range(parts):
        wanted = wanted_ref[part * size : (part + 1) * size, :]
        pick = (wanted == ids).astype(F32).astype(BF)
        chunk = rows_ref.at[part * chips : (part + 1) * chips]
        chunk[...] = dot(pick, coded).astype(BF).reshape(chunk.shape)
        copy = pltpu.make_async_copy(
            chunk, out_hbm.at[part * chips : (part + 1) * chips], out_sems.at[part]
        )
        copy.start()
        sent.append(copy)
    for copy in sent:
        copy.wait()


def outgoing_rows(place, target, wanted, hist, chips):
    rows, width = wanted.shape[0], hist.shape[1] // 2
    shape = (chips, NC, rows // chips // NC, width)
    parts = 4
    return pl.pallas_call(
        outgoing_kernel,
        out_shape=jax.ShapeDtypeStruct(shape, BF),
        in_specs=scalars() + whole(2) + far_off(1),
        out_specs=far_off(1)[0],
        scratch_shapes=room(hist)
        + [pltpu.VMEM(shape, BF), pltpu.SemaphoreType.DMA((parts,))],
        name="outgoing_rows",
        **grant(52, 2000000000, 6000000),
    )(place, target, wanted, hist)


def counts_kernel(slot_count, place_ref, links_ref, counts_ref):
    fanout, count = links_ref.shape
    size = (counts_ref.shape[0] - count) // NC
    local = lax.broadcasted_iota(jnp.int32, (count, count), 0)
    row = lax.broadcasted_iota(jnp.int32, (size, count), 0)
    core = place_ref[CORE]
    start = 0
    for ids in (
        local,
        (row // slot_count * NC + core) * slot_count + row % slot_count + count,
        (row // slot_count * NC + 1 - core) * slot_count + row % slot_count + count,
    ):
        total = jnp.zeros(ids.shape, F32)
        for neighbour in range(fanout):
            total = total + (links_ref[neighbour : neighbour + 1, :] == ids).astype(F32)
        counts_ref[start : start + ids.shape[0], :] = total.astype(BF)
        start += ids.shape[0]


def link_counts(place, links, peers, slot_count):
    count = links.shape[1]
    return pl.pallas_call(
        lambda *refs: counts_kernel(slot_count, *refs),
        out_shape=jax.ShapeDtypeStruct((count + peers * slot_count, count), BF),
        in_specs=scalars() + whole(1),
        out_specs=pl.BlockSpec(),
        name="link_counts",
        **grant(48, 4000000000, 2000000),
    )(place, links)


def halo_kernel(
    place_ref,
    target_hbm,
    counts_hbm,
    hist_hbm,
    received_hbm,
    across_hbm,
    sum_ref,
    texts_ref,
    target_ref,
    counts_ref,
    hist_ref,
    received_ref,
    across_ref,
    semaphores,
):
    core, me = place_ref[CORE], place_ref[ME]
    chips, slot_count, width = received_ref.shape
    size = chips * slot_count
    count = hist_ref.shape[0]
    copies = fetch(
        (target_hbm, counts_hbm, hist_hbm, received_hbm.at[:, core], across_hbm.at[:, core]),
        (target_ref, counts_ref, hist_ref, received_ref, across_ref),
        semaphores,
    )
    slots = slot_texts(target_ref.shape[1], chips, core, me)
    text_ids = lax.broadcasted_iota(jnp.int32, slots.shape, 1)
    copies[0].wait()
    place, row_text = text_rows(target_ref[...], count, place_ref[DOM])
    for copy in copies[1:]:
        copy.wait()
    near = counts_ref[:count, :]
    base = jnp.where(row_text >= 0, 0.0, sliced(hist_ref[...].astype(F32), me % 2, width))
    total = dot_t(near, base.astype(BF))
    counts_slot = dot_t(near, (row_text == slots).astype(F32).astype(BF))
    counts_text = dot_t(near, place)
    for k, ref in enumerate((received_ref, across_ref)):
        received = ref[...].reshape(size, width)
        first = received[:, 0:128].astype(F32)
        is_text = first[:, 0:1] > 24
        text = ((first[:, 0:1] - 32) * 16 + first[:, 1:2] - 32).astype(jnp.int32)
        text = jnp.where(is_text, text, -1)
        halo = received * jnp.where(is_text, 0.0, 1.0).astype(BF)
        far = counts_ref[count + k * size : count + (k + 1) * size, :]
        total = total + dot_t(far, halo)
        counts_slot = counts_slot + dot_t(far, (text == slots).astype(F32).astype(BF))
        counts_text = counts_text + dot_t(far, (text == text_ids).astype(F32).astype(BF))
    sum_ref[...] = total.astype(BF)
    texts_ref[0] = counts_slot.astype(BF)
    texts_ref[1] = counts_text.astype(BF)


def halo_sums(place, received, across, target, counts, hist):
    count = hist.shape[0]
    square = jax.ShapeDtypeStruct((2, count, target.shape[1]), BF)
    rows = pltpu.VMEM((received.shape[0],) + received.shape[2:], BF)
    return pl.pallas_call(
        halo_kernel,
        out_shape=(jax.ShapeDtypeStruct((count, received.shape[3]), BF), square),
        in_specs=scalars() + far_off(5),
        out_specs=(pl.BlockSpec(),) * 2,
        scratch_shapes=room(target, counts, hist)[:-1]
        + [rows, rows, pltpu.SemaphoreType.DMA((5,))],
        name="halo_sums",
        **grant(32, 1000000000, 5000000),
    )(place, target, counts, hist, received, across)


def head_kernel(fanout, place_ref, fresh_ref, *refs):
    sources, semaphores, (counts_ref, sums_ref, got_ref, hist_ref, target_ref, up_ref) = (
        refs[:8],
        refs[-7],
        refs[-6:],
    )
    table_ref, agg_ref, other_ref, texts_ref, w_self_ref, w_neigh_ref, upstream_ref = refs[8:-7]
    target_hbm, counts_hbm, sums_hbm, got_hbm, hist_hbm, w_self_hbm, w_neigh_hbm, up_hbm = sources
    copies = fetch(
        (
            counts_hbm.at[0],
            sums_hbm,
            got_hbm,
            target_hbm,
            hist_hbm,
            up_hbm,
            counts_hbm.at[1],
            w_self_hbm,
            w_neigh_hbm,
        ),
        (
            counts_ref,
            sums_ref,
            got_ref,
            target_ref,
            hist_ref,
            up_ref,
            texts_ref.at[1],
            w_self_ref,
            w_neigh_ref,
        ),
        semaphores,
    )
    half = fresh_ref.shape[0]
    count = hist_ref.shape[0]
    fresh = fresh_ref[...]
    for copy in copies[:3]:
        copy.wait()
    first, second = sums_ref[...].astype(F32), got_ref[...].astype(F32)
    low = place_ref[ME] % 2 == 0
    sums = [jnp.where(low, first, second), jnp.where(low, second, first)]
    agg_ref[...] = jnp.concatenate(sums, axis=1) + dot(counts_ref[:, :half], fresh)
    other_ref[1] = counts_ref[:, half:]
    copies[3].wait()
    place, row_text = text_rows(target_ref[...], count, place_ref[DOM])
    texts_ref[0] = place
    slots = slot_texts(place.shape[1], half // NY, place_ref[CORE], place_ref[ME])
    place_slot = (row_text == slots).astype(F32).astype(BF)
    other_ref[0] = place_slot[:, half:]
    placed = dot(place_slot[:, :half], fresh)
    copies[4].wait()
    table_ref[...] = jnp.where(row_text >= 0, placed, hist_ref[...].astype(F32)).astype(BF)
    copies[5].wait()
    upstream_ref[...] = up_ref[...].astype(F32).T
    for copy in copies[6:]:
        copy.wait()


def sage_head(place, fresh, counts, sums, target, hist, w_self, w_neigh, upstream, fanout):
    _, count, texts = counts.shape
    return pl.pallas_call(
        lambda *refs: head_kernel(fanout, *refs),
        out_shape=(
            jax.ShapeDtypeStruct(hist.shape, BF),
            jax.ShapeDtypeStruct(hist.shape, F32),
            jax.ShapeDtypeStruct((2, count, texts - fresh.shape[0]), BF),
            jax.ShapeDtypeStruct((2, count, texts), BF),
            jax.ShapeDtypeStruct(w_self.shape, BF),
            jax.ShapeDtypeStruct(w_neigh.shape, BF),
            jax.ShapeDtypeStruct(upstream.shape[::-1], F32),
        ),
        in_specs=scalars() + whole(1) + far_off(8),
        out_specs=tuple(whole(7)),
        scratch_shapes=[
            pltpu.SemaphoreType.DMA((9,)),
            pltpu.VMEM((count, texts), BF),
            pltpu.VMEM(sums[0].shape, BF),
            pltpu.VMEM(sums[1].shape, BF),
            pltpu.VMEM(hist.shape, BF),
            pltpu.VMEM(target.shape, jnp.int32),
            pltpu.VMEM(upstream.shape, BF),
        ],
        name="sage_head",
        **grant(48, 3000000000, 4000000),
    )(place, fresh, target, counts, *sums, hist, w_self, w_neigh, upstream)


def sage_kernel(
    fanout,
    place_ref,
    fresh_ref,
    table_ref,
    agg_ref,
    other_ref,
    texts_ref,
    w_self_ref,
    w_neigh_ref,
    upstream_ref,
    act_ref,
    weights_ref,
    terms_ref,
    send_ref,
    blocks_ref,
):
    fresh = fresh_ref[...]
    quarter = w_self_ref.shape[0]
    table = table_ref[...] + dot(other_ref[0], fresh).astype(BF)
    agg_rows = ((agg_ref[...] + dot(other_ref[1], fresh)) / fanout).astype(BF)
    pre_act = dot_nt(table, w_self_ref[...]) + dot_nt(agg_rows, w_neigh_ref[...])
    cdf = 0.5 * (1.0 + lax.erf(pre_act * math.sqrt(0.5)))
    density = jnp.exp(-0.5 * pre_act * pre_act) * (1.0 / math.sqrt(2.0 * math.pi))
    act_ref[...] = pre_act * cdf
    grad_pre = (upstream_ref[...] * (cdf + pre_act * density)).astype(BF)
    chips = weights_ref.shape[0]
    for k, rows in enumerate((table, agg_rows)):
        part = slice(k * quarter, (k + 1) * quarter)
        weights_ref[:, :, part] = dot_t(rows, grad_pre).reshape(chips, -1, quarter)
        terms_ref[:, :, part] = dot_t(texts_ref[k], grad_pre).reshape(chips, -1, quarter)
    put_blocks(1 - place_ref[CORE], weights_ref, terms_ref, blocks_ref)
    send_ref[...] = blocks_ref[...].astype(BF)


def put_blocks(side, weights_ref, terms_ref, blocks_ref):
    share, own_texts = weights_ref.shape[1] // NC, terms_ref.shape[1] // NC
    for core in range(NC):

        @pl.when(side == core)
        def _():
            rows = slice(core * share, (core + 1) * share)
            blocks_ref[:, :share, :] = weights_ref[:, rows, :]
            rows = slice(core * own_texts, (core + 1) * own_texts)
            blocks_ref[:, share:, :] = terms_ref[:, rows, :]


def sage(place, fresh, table, agg, other, texts, w_self, w_neigh, upstream, fanout, chips):
    quarter, width = w_self.shape
    count = table.shape[0]
    share, own_texts = width // chips, texts.shape[2] // chips
    block = (chips, (share + own_texts) // NC, 2 * quarter)
    return pl.pallas_call(
        lambda *refs: sage_kernel(fanout, *refs),
        out_shape=(
            jax.ShapeDtypeStruct((count, quarter), F32),
            jax.ShapeDtypeStruct((chips, share, 2 * quarter), F32),
            jax.ShapeDtypeStruct((chips, own_texts, 2 * quarter), F32),
            jax.ShapeDtypeStruct(block, BF),
        ),
        in_specs=scalars() + whole(8),
        out_specs=tuple(whole(4)),
        scratch_shapes=[pltpu.VMEM(block, F32)],
        name="sage",
        **grant(16, 2000000000, 8000000),
    )(place, fresh, table, agg, other, texts, w_self, w_neigh, upstream)


def tail_kernel(place_ref, act_ref, weights_ref, terms_ref, sage_ref, keep_ref):
    sage_ref[...] = act_ref[...].T.astype(BF)
    put_blocks(place_ref[CORE], weights_ref, terms_ref, keep_ref)


def sage_tail(place, act, weights, terms, send):
    return pl.pallas_call(
        tail_kernel,
        out_shape=(
            jax.ShapeDtypeStruct(act.shape[::-1], BF),
            jax.ShapeDtypeStruct(send.shape, F32),
        ),
        in_specs=scalars() + whole(3),
        out_specs=tuple(whole(2)),
        name="sage_tail",
        **grant(16, 3000000000, 4000000),
    )(place, act, weights, terms)


def combine_kernel(keep_ref, got_ref, out_ref):
    sums = keep_ref[...] + got_ref[...].astype(F32)
    out_ref[...] = sums.astype(BF)


def combine(keep, got):
    return pl.pallas_call(
        combine_kernel,
        out_shape=jax.ShapeDtypeStruct(got.shape, BF),
        in_specs=whole(2),
        out_specs=whole(1)[0],
        name="combine",
        **grant(16, 200000, 1200000),
    )(keep, got)


def final_kernel(fanout, share, place_ref, parts_ref, w_self_ref, w_neigh_ref, *term_refs):
    quarter = w_self_ref.shape[0]
    rows = jnp.sum(parts_ref[...].astype(F32), axis=0)[share:]
    at_rows = rows[:, :quarter].astype(BF)
    at_links = (rows[:, quarter:] / fanout).astype(BF)
    terms = dot(at_rows, w_self_ref[...]) + dot(at_links, w_neigh_ref[...])
    for s, ref in enumerate(term_refs):
        ref[...] = sliced(terms, lax.rem(place_ref[ME] + s, NY), quarter)


def final_terms(place, parts, w_self, w_neigh, share, fanout):
    quarter = w_self.shape[0]
    texts = jax.ShapeDtypeStruct((parts.shape[1] - share, quarter), F32)
    return pl.pallas_call(
        lambda *refs: final_kernel(fanout, share, *refs),
        out_shape=(texts,) * NY,
        in_specs=scalars() + whole(3),
        out_specs=tuple(whole(NY)),
        name="final_terms",
        **grant(16, 10000000, 1000000),
    )(place, parts, w_self, w_neigh)


def weight_kernel(parts_ref, self_ref, neigh_ref):
    share, quarter = self_ref.shape
    total = jnp.sum(parts_ref[...].astype(F32), axis=0)
    self_ref[...] = total[:share, :quarter]
    neigh_ref[...] = total[:share, quarter:]


def final_weights(parts, share):
    grads = jax.ShapeDtypeStruct((share, parts.shape[2] // 2), F32)
    return pl.pallas_call(
        weight_kernel,
        out_shape=(grads, grads),
        in_specs=whole(1),
        out_specs=(pl.BlockSpec(),) * 2,
        name="final_weights",
        **grant(16, 3000000000, 4000000),
    )(parts)


def local(
    hidden_states,
    text_len,
    w_qkv,
    w_out,
    w_up,
    w_down,
    hist,
    nbr,
    send_rows,
    fresh_target,
    w_self,
    w_neigh,
    upstream,
):
    my_x, my_z, my_c, my_y = (lax.axis_index(axis) for axis in "xzcy")
    model_width = hist.shape[1]
    peer_count, slot_count = send_rows.shape[1:]
    fanout = nbr.shape[1]
    share = model_width // peer_count
    chips = peer_count // NC
    dom = (my_x * NZ + my_z) * NC + my_c

    texts = (NY, hidden_states.shape[0] // NY, model_width)
    context = attend(hidden_states, text_len, w_qkv)
    attended = dot(context, w_out).astype(BF).reshape(texts)

    def part(s):
        return lax.dynamic_index_in_dim(attended, (my_y + s) % NY, 0, keepdims=False)

    residual = lax.dynamic_index_in_dim(hidden_states.reshape(texts), my_y, 0, keepdims=False)
    parts = [part(0)] + [pull(part(NY - s), "y", s) for s in (2, 1, 3)]
    first_norm = first_layer_norm(residual, parts)

    target = fresh_target[None, :]
    attended, wanted, lengths = lax.optimization_barrier((attended, send_rows, text_len))
    place = jnp.concatenate([jnp.stack([dom, my_c, my_y]).astype(jnp.int32), lengths])
    wanted = wanted.reshape(peer_count * slot_count, 1)
    outgoing = outgoing_rows(place, target, wanted, hist, chips)
    received = lax.all_to_all(outgoing, ("x", "z"), split_axis=0, concat_axis=0, tiled=True)

    others = {s: pull(first_norm, "y", s) for s in (1, 3, 2)}
    own, up, down = feed_first(first_norm, w_up, w_down)
    up, late_nbr = lax.optimization_barrier((up, nbr))
    linked = link_counts(place, late_nbr.T, peer_count, slot_count)
    others[2], linked = lax.optimization_barrier((others[2], linked))
    parts = [own] + [pull(feed(others[s], up, down), "y", NY - s) for s in (1, 3, 2)]
    fresh_row = pooled_row(place, first_norm, parts)

    rows = [fresh_row] + [pull(fresh_row, "y", s) for s in (1, 3, 2)]
    _, received = lax.optimization_barrier((fresh_row, received))
    across = pull(received, "c", 1)
    sums, counts = halo_sums(place, received, across, target, linked, hist)
    rows, sums, counts = lax.optimization_barrier((rows, sums, counts))
    rows = spread_rows(rows, chips)
    fresh = lax.all_to_all(rows, ("x", "z"), split_axis=0, concat_axis=0, tiled=True)
    sums = (sums, swap(sums))
    fresh, sums = lax.optimization_barrier((fresh, sums))
    fresh = fresh.reshape(-1, model_width)
    other = pull(fresh, "c", 1)

    begun = sage_head(
        place, fresh, counts, sums, target, hist, w_self.T, w_neigh.T, upstream.T, fanout
    )
    act, weights, terms, send = sage(place, other, *begun, fanout, chips)
    sage_out, keep = sage_tail(place, act, weights, terms, send)
    parts = combine(keep, pull(send, "c", 1))
    parts = lax.all_to_all(parts, ("x", "z"), split_axis=0, concat_axis=0, tiled=True)
    grad_fresh, *terms = final_terms(place, parts, w_self.T, w_neigh.T, share, fanout)
    grad_self_w, grad_neigh_w = final_weights(parts, share)
    for s in (2, 1, 3):
        grad_fresh = grad_fresh + pull(terms[NY - s - 1], "y", s)
    return (sage_out.T, grad_fresh, grad_self_w, grad_neigh_w)


def solution(mesh):
    dom = ("x", "z", "c")
    split = Mesh(mesh.devices.reshape(NX, NZ, NC, NY), dom + ("y",))
    in_specs = (
        P(dom, None),
        P(dom),
        P(None, None, "y"),
        P("y", None),
        P(None, "y"),
        P("y", None),
        P(dom, None),
        P(dom, None),
        P(dom, None, None),
        P(),
        P(None, "y"),
        P(None, "y"),
        P(dom, "y"),
    )
    out_specs = (P(dom, "y"),) * 4
    return jax.shard_map(local, mesh=split, in_specs=in_specs, out_specs=out_specs, check_vma=False)
```

```python
import math

import jax
import jax.numpy as jnp
from jax import lax
from jax.experimental import pallas as pl
from jax.experimental.pallas import tpu as pltpu
from jax.sharding import Mesh, PartitionSpec as P

HEADS = 12
EPSILON = 1e-05
NX, NZ, NC, NY = 4, 8, 2, 4
BF = jnp.bfloat16
F32 = jnp.float32


def layer_norm(values):
    center = values - jnp.mean(values, axis=-1, keepdims=True)
    spread = jnp.mean(center * center, axis=-1, keepdims=True)
    return center * lax.rsqrt(spread + EPSILON)


def exact_gelu(values):
    return 0.5 * values * (1.0 + lax.erf(values * math.sqrt(0.5)))


def dot(a, b):
    return jnp.dot(a, b, preferred_element_type=F32)


def dot_t(a, b):
    return lax.dot_general(a, b, (((0,), (0,)), ((), ())), preferred_element_type=F32)


def dot_nt(a, b):
    return lax.dot_general(a, b, (((1,), (1,)), ((), ())), preferred_element_type=F32)


def swap(value):
    return lax.ppermute(value, "y", [(i, i ^ 1) for i in range(NY)])


def pull(value, axis, shift):
    count = {"x": NX, "z": NZ, "c": NC, "y": NY}[axis]
    return lax.ppermute(value, axis, [((i + shift) % count, i) for i in range(count)])


def whole(count):
    return [pl.BlockSpec(memory_space=pltpu.VMEM)] * count


def far_off(count):
    return [pl.BlockSpec(memory_space=pltpu.HBM)] * count


def scalars():
    return [pl.BlockSpec(memory_space=pltpu.SMEM)]


def grant(mib, flops, bytes_accessed):
    return {
        "compiler_params": pltpu.CompilerParams(vmem_limit_bytes=mib * 2**20),
        "cost_estimate": pl.CostEstimate(
            flops=flops, bytes_accessed=bytes_accessed, transcendentals=0
        ),
    }


def room(*arrays):
    return [pltpu.VMEM(a.shape, a.dtype) for a in arrays] + [pltpu.SemaphoreType.DMA((len(arrays),))]


def fetch(sources, targets, semaphores):
    copies = [
        pltpu.make_async_copy(source, target, semaphores.at[k])
        for k, (source, target) in enumerate(zip(sources, targets))
    ]
    for copy in copies:
        copy.start()
    return copies


DOM, CORE, ME, LENGTHS = 0, 1, 2, 3


def attend(rows, lengths, weights_qkv):
    model_width = rows.shape[1]
    text_count = lengths.shape[0]
    length = rows.shape[0] // text_count
    local_width = weights_qkv.shape[2]
    head_dim = model_width // HEADS
    head_count = local_width // head_dim
    packed = dot(rows, weights_qkv.reshape(model_width, 3 * local_width)).astype(BF)
    packed = packed.reshape(text_count, length, 3, head_count, head_dim)
    scores = jnp.einsum(
        "tqhc,tkhc->thqk", packed[:, :, 0], packed[:, :, 1], preferred_element_type=F32
    ) / math.sqrt(head_dim)
    live_keys = jnp.arange(length)[None, :] < lengths[:, None]
    scores = jnp.where(live_keys[:, None, None, :], scores, -1e30)
    row_peak = jnp.max(scores, axis=-1, keepdims=True)
    weights = jnp.exp(scores - row_peak)
    attention_probs = (weights / jnp.sum(weights, axis=-1, keepdims=True)).astype(BF)
    context = jnp.einsum(
        "thqk,tkhc->tqhc", attention_probs, packed[:, :, 2], preferred_element_type=F32
    )
    return context.astype(BF).reshape(text_count * length, local_width)


def norm_kernel(residual_ref, own_ref, near_ref, far_ref, across_ref, out_ref):
    total = residual_ref[...].astype(F32) + own_ref[...].astype(F32)
    for ref in (near_ref, far_ref, across_ref):
        total = total + ref[...].astype(F32)
    out_ref[...] = layer_norm(total).astype(BF)


def first_layer_norm(residual, parts):
    return pl.pallas_call(
        norm_kernel,
        out_shape=jax.ShapeDtypeStruct(residual.shape, BF),
        in_specs=whole(5),
        out_specs=whole(1)[0],
        name="first_norm",
        **grant(16, 4000000000, 1200000),
    )(residual, *parts)


def feed_kernel(block_ref, up_ref, down_ref, out_ref):
    inner = exact_gelu(dot(block_ref[...], up_ref[...])).astype(BF)
    out_ref[...] = dot(inner, down_ref[...]).astype(out_ref.dtype)


def feed_first_kernel(block_ref, up_hbm, down_hbm, out_ref, up_ref, down_ref, semaphores):
    copies = fetch((up_hbm, down_hbm), (up_ref, down_ref), semaphores)
    copies[0].wait()
    inner = exact_gelu(dot(block_ref[...], up_ref[...])).astype(BF)
    copies[1].wait()
    out_ref[...] = dot(inner, down_ref[...])


def feed_first(block, w_up, w_down):
    return pl.pallas_call(
        feed_first_kernel,
        out_shape=(
            jax.ShapeDtypeStruct(block.shape, F32),
            jax.ShapeDtypeStruct(w_up.shape, BF),
            jax.ShapeDtypeStruct(w_down.shape, BF),
        ),
        in_specs=whole(1) + far_off(2),
        out_specs=tuple(whole(3)),
        scratch_shapes=[pltpu.SemaphoreType.DMA((2,))],
        name="feed_first",
        **grant(16, 8000000000, 9000000),
    )(block, w_up, w_down)


def feed(block, w_up, w_down):
    return pl.pallas_call(
        feed_kernel,
        out_shape=jax.ShapeDtypeStruct(block.shape, BF),
        in_specs=whole(3),
        out_specs=whole(1)[0],
        name="feed",
        **grant(16, 8000000000, 9000000),
    )(block, w_up, w_down)


def pool_kernel(place_ref, first_ref, own_ref, near_ref, far_ref, across_ref, out_ref):
    total = first_ref[...].astype(F32) + own_ref[...]
    for ref in (near_ref, far_ref, across_ref):
        total = total + ref[...].astype(F32)
    normed = layer_norm(total)
    length = place_ref[LENGTHS + place_ref[ME]]
    live = lax.broadcasted_iota(jnp.int32, normed.shape, 0) < length
    pooled = jnp.sum(jnp.where(live, normed, 0.0), axis=0, keepdims=True)
    out_ref[...] = (pooled / length.astype(F32)).astype(BF)


def pooled_row(place, first_norm, parts):
    return pl.pallas_call(
        pool_kernel,
        out_shape=jax.ShapeDtypeStruct((1, first_norm.shape[1]), BF),
        in_specs=scalars() + whole(5),
        out_specs=whole(1)[0],
        name="pooled_row",
        **grant(16, 4000000000, 1200000),
    )(place, first_norm, *parts)


def spread_kernel(own_ref, near_ref, far_ref, across_ref, out_ref):
    refs = (own_ref, near_ref, far_ref, across_ref)
    index = lax.broadcasted_iota(jnp.int32, out_ref.shape[1:], 0)
    rows = jnp.zeros(out_ref.shape[1:], F32)
    for s, ref in enumerate(refs):
        rows = jnp.where(index == s, ref[...].astype(F32), rows)
    out_ref[...] = jnp.broadcast_to(rows.astype(BF)[None], out_ref.shape)


def spread_rows(rows, chips):
    return pl.pallas_call(
        spread_kernel,
        out_shape=jax.ShapeDtypeStruct((chips, len(rows), rows[0].shape[1]), BF),
        in_specs=whole(len(rows)),
        out_specs=whole(1)[0],
        name="spread_rows",
        **grant(16, 1000000, 200000),
    )(*rows)


def sliced(values, index, width):
    total = values[:, :width]
    for k in range(1, values.shape[1] // width):
        total = jnp.where(index == k, values[:, k * width : (k + 1) * width], total)
    return total


def text_rows(target, count, dom):
    shape = (count, target.shape[1])
    row_ids = lax.broadcasted_iota(jnp.int32, shape, 0) + dom * count
    text_ids = lax.broadcasted_iota(jnp.int32, shape, 1)
    holds = row_ids == target
    row_text = jnp.sum(jnp.where(holds, text_ids + 1, 0), axis=1, keepdims=True) - 1
    return holds.astype(F32).astype(BF), row_text


def slot_texts(texts, chips, core, me):
    slot = lax.broadcasted_iota(jnp.int32, (1, texts), 1)
    step = slot % NY
    slot_y = ((step ^ (step >> 1)) + me) % NY
    slot_core = (slot // (chips * NY) + core) % NC
    return ((slot // NY % chips) * NC + slot_core) * NY + slot_y


def outgoing_kernel(
    place_ref, target_ref, wanted_ref, hist_ref, out_hbm, rows_ref, out_sems
):
    count, width = hist_ref.shape[0], rows_ref.shape[3]
    _, row_text = text_rows(target_ref[...], count, place_ref[DOM])
    column = lax.broadcasted_iota(jnp.int32, (count, width), 1)
    code = jnp.where(
        column == 0, 32 + row_text // 16, jnp.where(column == 1, 32 + row_text % 16, 0)
    ).astype(F32)
    parts = out_sems.shape[0]
    chips = rows_ref.shape[0] // parts
    size = wanted_ref.shape[0] // parts
    ids = lax.broadcasted_iota(jnp.int32, (size, count), 1)
    hist = sliced(hist_ref[...].astype(F32), place_ref[ME] % 2, width)
    coded = jnp.where(row_text >= 0, code, hist).astype(BF)
    sent = []
    for part in range(parts):
        wanted = wanted_ref[part * size : (part + 1) * size, :]
        pick = (wanted == ids).astype(F32).astype(BF)
        chunk = rows_ref.at[part * chips : (part + 1) * chips]
        chunk[...] = dot(pick, coded).astype(BF).reshape(chunk.shape)
        copy = pltpu.make_async_copy(
            chunk, out_hbm.at[part * chips : (part + 1) * chips], out_sems.at[part]
        )
        copy.start()
        sent.append(copy)
    for copy in sent:
        copy.wait()


def outgoing_rows(place, target, wanted, hist, chips):
    rows, width = wanted.shape[0], hist.shape[1] // 2
    shape = (chips, NC, rows // chips // NC, width)
    parts = 4
    return pl.pallas_call(
        outgoing_kernel,
        out_shape=jax.ShapeDtypeStruct(shape, BF),
        in_specs=scalars() + whole(3),
        out_specs=far_off(1)[0],
        scratch_shapes=[pltpu.VMEM(shape, BF), pltpu.SemaphoreType.DMA((parts,))],
        name="outgoing_rows",
        **grant(52, 2000000000, 6000000),
    )(place, target, wanted, hist)


def counts_kernel(slot_count, place_ref, links_ref, counts_ref):
    fanout, count = links_ref.shape
    size = (counts_ref.shape[0] - count) // NC
    local = lax.broadcasted_iota(jnp.int32, (count, count), 0)
    row = lax.broadcasted_iota(jnp.int32, (size, count), 0)
    core = place_ref[CORE]
    start = 0
    for ids in (
        local,
        (row // slot_count * NC + core) * slot_count + row % slot_count + count,
        (row // slot_count * NC + 1 - core) * slot_count + row % slot_count + count,
    ):
        total = jnp.zeros(ids.shape, F32)
        for neighbour in range(fanout):
            total = total + (links_ref[neighbour : neighbour + 1, :] == ids).astype(F32)
        counts_ref[start : start + ids.shape[0], :] = total.astype(BF)
        start += ids.shape[0]


def link_counts(place, links, peers, slot_count):
    count = links.shape[1]
    return pl.pallas_call(
        lambda *refs: counts_kernel(slot_count, *refs),
        out_shape=jax.ShapeDtypeStruct((count + peers * slot_count, count), BF),
        in_specs=scalars() + whole(1),
        out_specs=pl.BlockSpec(),
        name="link_counts",
        **grant(48, 4000000000, 2000000),
    )(place, links)


def halo_kernel(
    place_ref,
    target_hbm,
    counts_hbm,
    hist_hbm,
    received_hbm,
    across_hbm,
    sum_ref,
    texts_ref,
    target_ref,
    counts_ref,
    hist_ref,
    received_ref,
    across_ref,
    semaphores,
):
    core, me = place_ref[CORE], place_ref[ME]
    chips, slot_count, width = received_ref.shape
    size = chips * slot_count
    count = hist_ref.shape[0]
    copies = fetch(
        (target_hbm, counts_hbm, hist_hbm, received_hbm.at[:, core], across_hbm.at[:, core]),
        (target_ref, counts_ref, hist_ref, received_ref, across_ref),
        semaphores,
    )
    slots = slot_texts(target_ref.shape[1], chips, core, me)
    text_ids = lax.broadcasted_iota(jnp.int32, slots.shape, 1)
    copies[0].wait()
    place, row_text = text_rows(target_ref[...], count, place_ref[DOM])
    for copy in copies[1:]:
        copy.wait()
    near = counts_ref[:count, :]
    base = jnp.where(row_text >= 0, 0.0, sliced(hist_ref[...].astype(F32), me % 2, width))
    total = dot_t(near, base.astype(BF))
    counts_slot = dot_t(near, (row_text == slots).astype(F32).astype(BF))
    counts_text = dot_t(near, place)
    for k, ref in enumerate((received_ref, across_ref)):
        received = ref[...].reshape(size, width)
        first = received[:, 0:128].astype(F32)
        is_text = first[:, 0:1] > 24
        text = ((first[:, 0:1] - 32) * 16 + first[:, 1:2] - 32).astype(jnp.int32)
        text = jnp.where(is_text, text, -1)
        halo = received * jnp.where(is_text, 0.0, 1.0).astype(BF)
        far = counts_ref[count + k * size : count + (k + 1) * size, :]
        total = total + dot_t(far, halo)
        counts_slot = counts_slot + dot_t(far, (text == slots).astype(F32).astype(BF))
        counts_text = counts_text + dot_t(far, (text == text_ids).astype(F32).astype(BF))
    sum_ref[...] = total.astype(BF)
    texts_ref[0] = counts_slot.astype(BF)
    texts_ref[1] = counts_text.astype(BF)


def halo_sums(place, received, across, target, counts, hist):
    count = hist.shape[0]
    square = jax.ShapeDtypeStruct((2, count, target.shape[1]), BF)
    rows = pltpu.VMEM((received.shape[0],) + received.shape[2:], BF)
    return pl.pallas_call(
        halo_kernel,
        out_shape=(jax.ShapeDtypeStruct((count, received.shape[3]), BF), square),
        in_specs=scalars() + far_off(5),
        out_specs=(pl.BlockSpec(),) * 2,
        scratch_shapes=room(target, counts, hist)[:-1]
        + [rows, rows, pltpu.SemaphoreType.DMA((5,))],
        name="halo_sums",
        **grant(32, 1000000000, 5000000),
    )(place, target, counts, hist, received, across)


def head_kernel(fanout, place_ref, fresh_ref, *refs):
    sources, semaphores, (counts_ref, sums_ref, got_ref, hist_ref, target_ref, up_ref) = (
        refs[:8],
        refs[-7],
        refs[-6:],
    )
    table_ref, agg_ref, other_ref, texts_ref, w_self_ref, w_neigh_ref, upstream_ref = refs[8:-7]
    target_hbm, counts_hbm, sums_hbm, got_hbm, hist_hbm, w_self_hbm, w_neigh_hbm, up_hbm = sources
    copies = fetch(
        (
            counts_hbm.at[0],
            sums_hbm,
            got_hbm,
            target_hbm,
            hist_hbm,
            up_hbm,
            counts_hbm.at[1],
            w_self_hbm,
            w_neigh_hbm,
        ),
        (
            counts_ref,
            sums_ref,
            got_ref,
            target_ref,
            hist_ref,
            up_ref,
            texts_ref.at[1],
            w_self_ref,
            w_neigh_ref,
        ),
        semaphores,
    )
    half = fresh_ref.shape[0]
    count = hist_ref.shape[0]
    fresh = fresh_ref[...]
    for copy in copies[:3]:
        copy.wait()
    first, second = sums_ref[...].astype(F32), got_ref[...].astype(F32)
    low = place_ref[ME] % 2 == 0
    sums = [jnp.where(low, first, second), jnp.where(low, second, first)]
    agg_ref[...] = jnp.concatenate(sums, axis=1) + dot(counts_ref[:, :half], fresh)
    other_ref[1] = counts_ref[:, half:]
    copies[3].wait()
    place, row_text = text_rows(target_ref[...], count, place_ref[DOM])
    texts_ref[0] = place
    slots = slot_texts(place.shape[1], half // NY, place_ref[CORE], place_ref[ME])
    place_slot = (row_text == slots).astype(F32).astype(BF)
    other_ref[0] = place_slot[:, half:]
    placed = dot(place_slot[:, :half], fresh)
    copies[4].wait()
    table_ref[...] = jnp.where(row_text >= 0, placed, hist_ref[...].astype(F32)).astype(BF)
    copies[5].wait()
    upstream_ref[...] = up_ref[...].astype(F32).T
    for copy in copies[6:]:
        copy.wait()


def sage_head(place, fresh, counts, sums, target, hist, w_self, w_neigh, upstream, fanout):
    _, count, texts = counts.shape
    return pl.pallas_call(
        lambda *refs: head_kernel(fanout, *refs),
        out_shape=(
            jax.ShapeDtypeStruct(hist.shape, BF),
            jax.ShapeDtypeStruct(hist.shape, F32),
            jax.ShapeDtypeStruct((2, count, texts - fresh.shape[0]), BF),
            jax.ShapeDtypeStruct((2, count, texts), BF),
            jax.ShapeDtypeStruct(w_self.shape, BF),
            jax.ShapeDtypeStruct(w_neigh.shape, BF),
            jax.ShapeDtypeStruct(upstream.shape[::-1], F32),
        ),
        in_specs=scalars() + whole(1) + far_off(8),
        out_specs=tuple(whole(7)),
        scratch_shapes=[
            pltpu.SemaphoreType.DMA((9,)),
            pltpu.VMEM((count, texts), BF),
            pltpu.VMEM(sums[0].shape, BF),
            pltpu.VMEM(sums[1].shape, BF),
            pltpu.VMEM(hist.shape, BF),
            pltpu.VMEM(target.shape, jnp.int32),
            pltpu.VMEM(upstream.shape, BF),
        ],
        name="sage_head",
        **grant(48, 3000000000, 4000000),
    )(place, fresh, target, counts, *sums, hist, w_self, w_neigh, upstream)


def sage_kernel(
    fanout,
    place_ref,
    fresh_ref,
    table_ref,
    agg_ref,
    other_ref,
    texts_ref,
    w_self_ref,
    w_neigh_ref,
    upstream_ref,
    act_ref,
    weights_ref,
    terms_ref,
    send_ref,
    blocks_ref,
):
    fresh = fresh_ref[...]
    quarter = w_self_ref.shape[0]
    table = table_ref[...] + dot(other_ref[0], fresh).astype(BF)
    agg_rows = ((agg_ref[...] + dot(other_ref[1], fresh)) / fanout).astype(BF)
    pre_act = dot_nt(table, w_self_ref[...]) + dot_nt(agg_rows, w_neigh_ref[...])
    cdf = 0.5 * (1.0 + lax.erf(pre_act * math.sqrt(0.5)))
    density = jnp.exp(-0.5 * pre_act * pre_act) * (1.0 / math.sqrt(2.0 * math.pi))
    act_ref[...] = pre_act * cdf
    grad_pre = (upstream_ref[...] * (cdf + pre_act * density)).astype(BF)
    chips = weights_ref.shape[0]
    for k, rows in enumerate((table, agg_rows)):
        part = slice(k * quarter, (k + 1) * quarter)
        weights_ref[:, :, part] = dot_t(rows, grad_pre).reshape(chips, -1, quarter)
        terms_ref[:, :, part] = dot_t(texts_ref[k], grad_pre).reshape(chips, -1, quarter)
    put_blocks(1 - place_ref[CORE], weights_ref, terms_ref, blocks_ref)
    send_ref[...] = blocks_ref[...].astype(BF)


def put_blocks(side, weights_ref, terms_ref, blocks_ref):
    share, own_texts = weights_ref.shape[1] // NC, terms_ref.shape[1] // NC
    for core in range(NC):

        @pl.when(side == core)
        def _():
            rows = slice(core * share, (core + 1) * share)
            blocks_ref[:, :share, :] = weights_ref[:, rows, :]
            rows = slice(core * own_texts, (core + 1) * own_texts)
            blocks_ref[:, share:, :] = terms_ref[:, rows, :]


def sage(place, fresh, table, agg, other, texts, w_self, w_neigh, upstream, fanout, chips):
    quarter, width = w_self.shape
    count = table.shape[0]
    share, own_texts = width // chips, texts.shape[2] // chips
    block = (chips, (share + own_texts) // NC, 2 * quarter)
    return pl.pallas_call(
        lambda *refs: sage_kernel(fanout, *refs),
        out_shape=(
            jax.ShapeDtypeStruct((count, quarter), F32),
            jax.ShapeDtypeStruct((chips, share, 2 * quarter), F32),
            jax.ShapeDtypeStruct((chips, own_texts, 2 * quarter), F32),
            jax.ShapeDtypeStruct(block, BF),
        ),
        in_specs=scalars() + whole(8),
        out_specs=tuple(whole(4)),
        scratch_shapes=[pltpu.VMEM(block, F32)],
        name="sage",
        **grant(16, 2000000000, 8000000),
    )(place, fresh, table, agg, other, texts, w_self, w_neigh, upstream)


def tail_kernel(place_ref, act_ref, weights_ref, terms_ref, sage_ref, keep_ref):
    sage_ref[...] = act_ref[...].T.astype(BF)
    put_blocks(place_ref[CORE], weights_ref, terms_ref, keep_ref)


def sage_tail(place, act, weights, terms, send):
    return pl.pallas_call(
        tail_kernel,
        out_shape=(
            jax.ShapeDtypeStruct(act.shape[::-1], BF),
            jax.ShapeDtypeStruct(send.shape, F32),
        ),
        in_specs=scalars() + whole(3),
        out_specs=tuple(whole(2)),
        name="sage_tail",
        **grant(16, 3000000000, 4000000),
    )(place, act, weights, terms)


def combine_kernel(keep_ref, got_ref, out_ref):
    sums = keep_ref[...] + got_ref[...].astype(F32)
    out_ref[...] = sums.astype(BF)


def combine(keep, got):
    return pl.pallas_call(
        combine_kernel,
        out_shape=jax.ShapeDtypeStruct(got.shape, BF),
        in_specs=whole(2),
        out_specs=whole(1)[0],
        name="combine",
        **grant(16, 200000, 1200000),
    )(keep, got)


def final_kernel(fanout, share, place_ref, parts_ref, w_self_ref, w_neigh_ref, *term_refs):
    quarter = w_self_ref.shape[0]
    rows = jnp.sum(parts_ref[...].astype(F32), axis=0)[share:]
    at_rows = rows[:, :quarter].astype(BF)
    at_links = (rows[:, quarter:] / fanout).astype(BF)
    terms = dot(at_rows, w_self_ref[...]) + dot(at_links, w_neigh_ref[...])
    for s, ref in enumerate(term_refs):
        ref[...] = sliced(terms, lax.rem(place_ref[ME] + s, NY), quarter)


def final_terms(place, parts, w_self, w_neigh, share, fanout):
    quarter = w_self.shape[0]
    texts = jax.ShapeDtypeStruct((parts.shape[1] - share, quarter), F32)
    return pl.pallas_call(
        lambda *refs: final_kernel(fanout, share, *refs),
        out_shape=(texts,) * NY,
        in_specs=scalars() + whole(3),
        out_specs=tuple(whole(NY)),
        name="final_terms",
        **grant(16, 10000000, 1000000),
    )(place, parts, w_self, w_neigh)


def weight_kernel(parts_ref, self_ref, neigh_ref):
    share, quarter = self_ref.shape
    total = jnp.sum(parts_ref[...].astype(F32), axis=0)
    self_ref[...] = total[:share, :quarter]
    neigh_ref[...] = total[:share, quarter:]


def final_weights(parts, share):
    grads = jax.ShapeDtypeStruct((share, parts.shape[2] // 2), F32)
    return pl.pallas_call(
        weight_kernel,
        out_shape=(grads, grads),
        in_specs=whole(1),
        out_specs=(pl.BlockSpec(),) * 2,
        name="final_weights",
        **grant(16, 3000000000, 4000000),
    )(parts)


def local(
    hidden_states,
    text_len,
    w_qkv,
    w_out,
    w_up,
    w_down,
    hist,
    nbr,
    send_rows,
    fresh_target,
    w_self,
    w_neigh,
    upstream,
):
    my_x, my_z, my_c, my_y = (lax.axis_index(axis) for axis in "xzcy")
    model_width = hist.shape[1]
    peer_count, slot_count = send_rows.shape[1:]
    fanout = nbr.shape[1]
    share = model_width // peer_count
    chips = peer_count // NC
    dom = (my_x * NZ + my_z) * NC + my_c

    texts = (NY, hidden_states.shape[0] // NY, model_width)
    context = attend(hidden_states, text_len, w_qkv)
    attended = dot(context, w_out).astype(BF).reshape(texts)

    def part(s):
        return lax.dynamic_index_in_dim(attended, (my_y + s) % NY, 0, keepdims=False)

    residual = lax.dynamic_index_in_dim(hidden_states.reshape(texts), my_y, 0, keepdims=False)
    parts = [part(0)] + [pull(part(NY - s), "y", s) for s in (2, 1, 3)]
    first_norm = first_layer_norm(residual, parts)

    target = fresh_target[None, :]
    attended, wanted, lengths = lax.optimization_barrier((attended, send_rows, text_len))
    place = jnp.concatenate([jnp.stack([dom, my_c, my_y]).astype(jnp.int32), lengths])
    wanted = wanted.reshape(peer_count * slot_count, 1)
    outgoing = outgoing_rows(place, target, wanted, hist, chips)
    received = lax.all_to_all(outgoing, ("x", "z"), split_axis=0, concat_axis=0, tiled=True)

    others = {s: pull(first_norm, "y", s) for s in (1, 3, 2)}
    own, up, down = feed_first(first_norm, w_up, w_down)
    up, late_nbr = lax.optimization_barrier((up, nbr))
    linked = link_counts(place, late_nbr.T, peer_count, slot_count)
    others[2], linked = lax.optimization_barrier((others[2], linked))
    parts = [own] + [pull(feed(others[s], up, down), "y", NY - s) for s in (1, 3, 2)]
    fresh_row = pooled_row(place, first_norm, parts)

    rows = [fresh_row] + [pull(fresh_row, "y", s) for s in (1, 3, 2)]
    _, received = lax.optimization_barrier((fresh_row, received))
    across = pull(received, "c", 1)
    sums, counts = halo_sums(place, received, across, target, linked, hist)
    rows, sums, counts = lax.optimization_barrier((rows, sums, counts))
    rows = spread_rows(rows, chips)
    fresh = lax.all_to_all(rows, ("x", "z"), split_axis=0, concat_axis=0, tiled=True)
    sums = (sums, swap(sums))
    fresh, sums = lax.optimization_barrier((fresh, sums))
    fresh = fresh.reshape(-1, model_width)
    other = pull(fresh, "c", 1)

    begun = sage_head(
        place, fresh, counts, sums, target, hist, w_self.T, w_neigh.T, upstream.T, fanout
    )
    act, weights, terms, send = sage(place, other, *begun, fanout, chips)
    sage_out, keep = sage_tail(place, act, weights, terms, send)
    parts = combine(keep, pull(send, "c", 1))
    parts = lax.all_to_all(parts, ("x", "z"), split_axis=0, concat_axis=0, tiled=True)
    grad_fresh, *terms = final_terms(place, parts, w_self.T, w_neigh.T, share, fanout)
    grad_self_w, grad_neigh_w = final_weights(parts, share)
    for s in (2, 1, 3):
        grad_fresh = grad_fresh + pull(terms[NY - s - 1], "y", s)
    return (sage_out.T, grad_fresh, grad_self_w, grad_neigh_w)


def solution(mesh):
    dom = ("x", "z", "c")
    split = Mesh(mesh.devices.reshape(NX, NZ, NC, NY), dom + ("y",))
    in_specs = (
        P(dom, None),
        P(dom),
        P(None, None, "y"),
        P("y", None),
        P(None, "y"),
        P("y", None),
        P(dom, None),
        P(dom, None),
        P(dom, None, None),
        P(),
        P(None, "y"),
        P(None, "y"),
        P(dom, "y"),
    )
    out_specs = (P(dom, "y"),) * 4
    return jax.shard_map(local, mesh=split, in_specs=in_specs, out_specs=out_specs, check_vma=False)
```

```python
import math

import jax
import jax.numpy as jnp
from jax import lax
from jax.experimental import pallas as pl
from jax.experimental.pallas import tpu as pltpu
from jax.sharding import Mesh, PartitionSpec as P

HEADS = 12
EPSILON = 1e-05
NX, NZ, NC, NY = 4, 8, 2, 4
BF = jnp.bfloat16
F32 = jnp.float32


def layer_norm(values):
    center = values - jnp.mean(values, axis=-1, keepdims=True)
    spread = jnp.mean(center * center, axis=-1, keepdims=True)
    return center * lax.rsqrt(spread + EPSILON)


def exact_gelu(values):
    return 0.5 * values * (1.0 + lax.erf(values * math.sqrt(0.5)))


def dot(a, b):
    return jnp.dot(a, b, preferred_element_type=F32)


def dot_t(a, b):
    return lax.dot_general(a, b, (((0,), (0,)), ((), ())), preferred_element_type=F32)


def dot_nt(a, b):
    return lax.dot_general(a, b, (((1,), (1,)), ((), ())), preferred_element_type=F32)


def swap(value):
    return lax.ppermute(value, "y", [(i, i ^ 1) for i in range(NY)])


def pull(value, axis, shift):
    count = {"x": NX, "z": NZ, "c": NC, "y": NY}[axis]
    return lax.ppermute(value, axis, [((i + shift) % count, i) for i in range(count)])


def whole(count):
    return [pl.BlockSpec(memory_space=pltpu.VMEM)] * count


def far_off(count):
    return [pl.BlockSpec(memory_space=pltpu.HBM)] * count


def scalars():
    return [pl.BlockSpec(memory_space=pltpu.SMEM)]


def grant(mib, flops, bytes_accessed):
    return {
        "compiler_params": pltpu.CompilerParams(vmem_limit_bytes=mib * 2**20),
        "cost_estimate": pl.CostEstimate(
            flops=flops, bytes_accessed=bytes_accessed, transcendentals=0
        ),
    }


def room(*arrays):
    return [pltpu.VMEM(a.shape, a.dtype) for a in arrays] + [pltpu.SemaphoreType.DMA((len(arrays),))]


def fetch(sources, targets, semaphores):
    copies = [
        pltpu.make_async_copy(source, target, semaphores.at[k])
        for k, (source, target) in enumerate(zip(sources, targets))
    ]
    for copy in copies:
        copy.start()
    return copies


DOM, CORE, ME, LENGTHS = 0, 1, 2, 3


def attend(rows, lengths, weights_qkv):
    model_width = rows.shape[1]
    text_count = lengths.shape[0]
    length = rows.shape[0] // text_count
    local_width = weights_qkv.shape[2]
    head_dim = model_width // HEADS
    head_count = local_width // head_dim
    packed = dot(rows, weights_qkv.reshape(model_width, 3 * local_width)).astype(BF)
    packed = packed.reshape(text_count, length, 3, head_count, head_dim)
    scores = jnp.einsum(
        "tqhc,tkhc->thqk", packed[:, :, 0], packed[:, :, 1], preferred_element_type=F32
    ) / math.sqrt(head_dim)
    live_keys = jnp.arange(length)[None, :] < lengths[:, None]
    scores = jnp.where(live_keys[:, None, None, :], scores, -1e30)
    row_peak = jnp.max(scores, axis=-1, keepdims=True)
    weights = jnp.exp(scores - row_peak)
    attention_probs = (weights / jnp.sum(weights, axis=-1, keepdims=True)).astype(BF)
    context = jnp.einsum(
        "thqk,tkhc->tqhc", attention_probs, packed[:, :, 2], preferred_element_type=F32
    )
    return context.astype(BF).reshape(text_count * length, local_width)


def norm_kernel(residual_ref, own_ref, near_ref, far_ref, across_ref, out_ref):
    total = residual_ref[...].astype(F32) + own_ref[...].astype(F32)
    for ref in (near_ref, far_ref, across_ref):
        total = total + ref[...].astype(F32)
    out_ref[...] = layer_norm(total).astype(BF)


def first_layer_norm(residual, parts):
    return pl.pallas_call(
        norm_kernel,
        out_shape=jax.ShapeDtypeStruct(residual.shape, BF),
        in_specs=whole(5),
        out_specs=whole(1)[0],
        name="first_norm",
        **grant(16, 4000000000, 1200000),
    )(residual, *parts)


def feed_kernel(block_ref, up_ref, down_ref, out_ref):
    inner = exact_gelu(dot(block_ref[...], up_ref[...])).astype(BF)
    out_ref[...] = dot(inner, down_ref[...]).astype(out_ref.dtype)


def feed_first_kernel(block_ref, up_hbm, down_hbm, out_ref, up_ref, down_ref, semaphores):
    copies = fetch((up_hbm, down_hbm), (up_ref, down_ref), semaphores)
    copies[0].wait()
    inner = exact_gelu(dot(block_ref[...], up_ref[...])).astype(BF)
    copies[1].wait()
    out_ref[...] = dot(inner, down_ref[...])


def feed_first(block, w_up, w_down):
    return pl.pallas_call(
        feed_first_kernel,
        out_shape=(
            jax.ShapeDtypeStruct(block.shape, F32),
            jax.ShapeDtypeStruct(w_up.shape, BF),
            jax.ShapeDtypeStruct(w_down.shape, BF),
        ),
        in_specs=whole(1) + far_off(2),
        out_specs=tuple(whole(3)),
        scratch_shapes=[pltpu.SemaphoreType.DMA((2,))],
        name="feed_first",
        **grant(16, 8000000000, 9000000),
    )(block, w_up, w_down)


def feed(block, w_up, w_down):
    return pl.pallas_call(
        feed_kernel,
        out_shape=jax.ShapeDtypeStruct(block.shape, BF),
        in_specs=whole(3),
        out_specs=whole(1)[0],
        name="feed",
        **grant(16, 8000000000, 9000000),
    )(block, w_up, w_down)


def pool_kernel(place_ref, first_ref, own_ref, near_ref, far_ref, across_ref, out_ref):
    total = first_ref[...].astype(F32) + own_ref[...]
    for ref in (near_ref, far_ref, across_ref):
        total = total + ref[...].astype(F32)
    normed = layer_norm(total)
    length = place_ref[LENGTHS + place_ref[ME]]
    live = lax.broadcasted_iota(jnp.int32, normed.shape, 0) < length
    pooled = jnp.sum(jnp.where(live, normed, 0.0), axis=0, keepdims=True)
    out_ref[...] = (pooled / length.astype(F32)).astype(BF)


def pooled_row(place, first_norm, parts):
    return pl.pallas_call(
        pool_kernel,
        out_shape=jax.ShapeDtypeStruct((1, first_norm.shape[1]), BF),
        in_specs=scalars() + whole(5),
        out_specs=whole(1)[0],
        name="pooled_row",
        **grant(16, 4000000000, 1200000),
    )(place, first_norm, *parts)


def spread_kernel(own_ref, near_ref, far_ref, across_ref, out_ref):
    refs = (own_ref, near_ref, far_ref, across_ref)
    index = lax.broadcasted_iota(jnp.int32, out_ref.shape[1:], 0)
    rows = jnp.zeros(out_ref.shape[1:], F32)
    for s, ref in enumerate(refs):
        rows = jnp.where(index == s, ref[...].astype(F32), rows)
    out_ref[...] = jnp.broadcast_to(rows.astype(BF)[None], out_ref.shape)


def spread_rows(rows, chips):
    return pl.pallas_call(
        spread_kernel,
        out_shape=jax.ShapeDtypeStruct((chips, len(rows), rows[0].shape[1]), BF),
        in_specs=whole(len(rows)),
        out_specs=whole(1)[0],
        name="spread_rows",
        **grant(16, 1000000, 200000),
    )(*rows)


def sliced(values, index, width):
    total = values[:, :width]
    for k in range(1, values.shape[1] // width):
        total = jnp.where(index == k, values[:, k * width : (k + 1) * width], total)
    return total


def text_rows(target, count, dom):
    shape = (count, target.shape[1])
    row_ids = lax.broadcasted_iota(jnp.int32, shape, 0) + dom * count
    text_ids = lax.broadcasted_iota(jnp.int32, shape, 1)
    holds = row_ids == target
    row_text = jnp.sum(jnp.where(holds, text_ids + 1, 0), axis=1, keepdims=True) - 1
    return holds.astype(F32).astype(BF), row_text


def slot_texts(texts, chips, core, me):
    slot = lax.broadcasted_iota(jnp.int32, (1, texts), 1)
    step = slot % NY
    slot_y = ((step ^ (step >> 1)) + me) % NY
    slot_core = (slot // (chips * NY) + core) % NC
    return ((slot // NY % chips) * NC + slot_core) * NY + slot_y


def outgoing_kernel(
    place_ref, target_ref, wanted_ref, hist_ref, out_hbm, rows_ref, out_sems
):
    count, width = hist_ref.shape[0], rows_ref.shape[3]
    _, row_text = text_rows(target_ref[...], count, place_ref[DOM])
    column = lax.broadcasted_iota(jnp.int32, (count, width), 1)
    code = jnp.where(
        column == 0, 32 + row_text // 16, jnp.where(column == 1, 32 + row_text % 16, 0)
    ).astype(F32)
    parts = out_sems.shape[0]
    chips = rows_ref.shape[0] // parts
    size = wanted_ref.shape[0] // parts
    ids = lax.broadcasted_iota(jnp.int32, (size, count), 1)
    hist = sliced(hist_ref[...].astype(F32), place_ref[ME] % 2, width)
    coded = jnp.where(row_text >= 0, code, hist).astype(BF)
    sent = []
    for part in range(parts):
        wanted = wanted_ref[part * size : (part + 1) * size, :]
        pick = (wanted == ids).astype(F32).astype(BF)
        chunk = rows_ref.at[part * chips : (part + 1) * chips]
        chunk[...] = dot(pick, coded).astype(BF).reshape(chunk.shape)
        copy = pltpu.make_async_copy(
            chunk, out_hbm.at[part * chips : (part + 1) * chips], out_sems.at[part]
        )
        copy.start()
        sent.append(copy)
    for copy in sent:
        copy.wait()


def outgoing_rows(place, target, wanted, hist, chips):
    rows, width = wanted.shape[0], hist.shape[1] // 2
    shape = (chips, NC, rows // chips // NC, width)
    parts = 4
    return pl.pallas_call(
        outgoing_kernel,
        out_shape=jax.ShapeDtypeStruct(shape, BF),
        in_specs=scalars() + whole(3),
        out_specs=far_off(1)[0],
        scratch_shapes=[pltpu.VMEM(shape, BF), pltpu.SemaphoreType.DMA((parts,))],
        name="outgoing_rows",
        **grant(52, 2000000000, 6000000),
    )(place, target, wanted, hist)


def counts_kernel(slot_count, place_ref, links_ref, counts_ref):
    fanout, count = links_ref.shape
    size = (counts_ref.shape[0] - count) // NC
    local = lax.broadcasted_iota(jnp.int32, (count, count), 0)
    row = lax.broadcasted_iota(jnp.int32, (size, count), 0)
    core = place_ref[CORE]
    start = 0
    for ids in (
        local,
        (row // slot_count * NC + core) * slot_count + row % slot_count + count,
        (row // slot_count * NC + 1 - core) * slot_count + row % slot_count + count,
    ):
        total = jnp.zeros(ids.shape, F32)
        for neighbour in range(fanout):
            total = total + (links_ref[neighbour : neighbour + 1, :] == ids).astype(F32)
        counts_ref[start : start + ids.shape[0], :] = total.astype(BF)
        start += ids.shape[0]


def link_counts(place, links, peers, slot_count):
    count = links.shape[1]
    return pl.pallas_call(
        lambda *refs: counts_kernel(slot_count, *refs),
        out_shape=jax.ShapeDtypeStruct((count + peers * slot_count, count), BF),
        in_specs=scalars() + whole(1),
        out_specs=pl.BlockSpec(),
        name="link_counts",
        **grant(48, 4000000000, 2000000),
    )(place, links)


def halo_kernel(
    place_ref,
    target_hbm,
    counts_hbm,
    hist_hbm,
    received_hbm,
    across_hbm,
    sum_ref,
    texts_ref,
    target_ref,
    counts_ref,
    hist_ref,
    received_ref,
    across_ref,
    semaphores,
):
    core, me = place_ref[CORE], place_ref[ME]
    chips, slot_count, width = received_ref.shape
    size = chips * slot_count
    count = hist_ref.shape[0]
    copies = fetch(
        (target_hbm, counts_hbm, hist_hbm, received_hbm.at[:, core], across_hbm.at[:, core]),
        (target_ref, counts_ref, hist_ref, received_ref, across_ref),
        semaphores,
    )
    slots = slot_texts(target_ref.shape[1], chips, core, me)
    text_ids = lax.broadcasted_iota(jnp.int32, slots.shape, 1)
    copies[0].wait()
    place, row_text = text_rows(target_ref[...], count, place_ref[DOM])
    for copy in copies[1:]:
        copy.wait()
    near = counts_ref[:count, :]
    base = jnp.where(row_text >= 0, 0.0, sliced(hist_ref[...].astype(F32), me % 2, width))
    total = dot_t(near, base.astype(BF))
    counts_slot = dot_t(near, (row_text == slots).astype(F32).astype(BF))
    counts_text = dot_t(near, place)
    for k, ref in enumerate((received_ref, across_ref)):
        received = ref[...].reshape(size, width)
        first = received[:, 0:128].astype(F32)
        is_text = first[:, 0:1] > 24
        text = ((first[:, 0:1] - 32) * 16 + first[:, 1:2] - 32).astype(jnp.int32)
        text = jnp.where(is_text, text, -1)
        halo = received * jnp.where(is_text, 0.0, 1.0).astype(BF)
        far = counts_ref[count + k * size : count + (k + 1) * size, :]
        total = total + dot_t(far, halo)
        counts_slot = counts_slot + dot_t(far, (text == slots).astype(F32).astype(BF))
        counts_text = counts_text + dot_t(far, (text == text_ids).astype(F32).astype(BF))
    sum_ref[...] = total.astype(BF)
    texts_ref[0] = counts_slot.astype(BF)
    texts_ref[1] = counts_text.astype(BF)


def halo_sums(place, received, across, target, counts, hist):
    count = hist.shape[0]
    square = jax.ShapeDtypeStruct((2, count, target.shape[1]), BF)
    rows = pltpu.VMEM((received.shape[0],) + received.shape[2:], BF)
    return pl.pallas_call(
        halo_kernel,
        out_shape=(jax.ShapeDtypeStruct((count, received.shape[3]), BF), square),
        in_specs=scalars() + far_off(5),
        out_specs=(pl.BlockSpec(),) * 2,
        scratch_shapes=room(target, counts, hist)[:-1]
        + [rows, rows, pltpu.SemaphoreType.DMA((5,))],
        name="halo_sums",
        **grant(32, 1000000000, 5000000),
    )(place, target, counts, hist, received, across)


def head_kernel(fanout, place_ref, fresh_ref, *refs):
    sources, semaphores, (counts_ref, sums_ref, got_ref, hist_ref, target_ref, up_ref) = (
        refs[:8],
        refs[-7],
        refs[-6:],
    )
    table_ref, agg_ref, other_ref, texts_ref, w_self_ref, w_neigh_ref, upstream_ref = refs[8:-7]
    target_hbm, counts_hbm, sums_hbm, got_hbm, hist_hbm, w_self_hbm, w_neigh_hbm, up_hbm = sources
    copies = fetch(
        (
            counts_hbm.at[0],
            sums_hbm,
            got_hbm,
            target_hbm,
            hist_hbm,
            up_hbm,
            counts_hbm.at[1],
            w_self_hbm,
            w_neigh_hbm,
        ),
        (
            counts_ref,
            sums_ref,
            got_ref,
            target_ref,
            hist_ref,
            up_ref,
            texts_ref.at[1],
            w_self_ref,
            w_neigh_ref,
        ),
        semaphores,
    )
    half = fresh_ref.shape[0]
    count = hist_ref.shape[0]
    fresh = fresh_ref[...]
    for copy in copies[:3]:
        copy.wait()
    first, second = sums_ref[...].astype(F32), got_ref[...].astype(F32)
    low = place_ref[ME] % 2 == 0
    sums = [jnp.where(low, first, second), jnp.where(low, second, first)]
    agg_ref[...] = jnp.concatenate(sums, axis=1) + dot(counts_ref[:, :half], fresh)
    other_ref[1] = counts_ref[:, half:]
    copies[3].wait()
    place, row_text = text_rows(target_ref[...], count, place_ref[DOM])
    texts_ref[0] = place
    slots = slot_texts(place.shape[1], half // NY, place_ref[CORE], place_ref[ME])
    place_slot = (row_text == slots).astype(F32).astype(BF)
    other_ref[0] = place_slot[:, half:]
    placed = dot(place_slot[:, :half], fresh)
    copies[4].wait()
    table_ref[...] = jnp.where(row_text >= 0, placed, hist_ref[...].astype(F32)).astype(BF)
    copies[5].wait()
    upstream_ref[...] = up_ref[...]
    for copy in copies[6:]:
        copy.wait()


def sage_head(place, fresh, counts, sums, target, hist, w_self, w_neigh, upstream, fanout):
    _, count, texts = counts.shape
    return pl.pallas_call(
        lambda *refs: head_kernel(fanout, *refs),
        out_shape=(
            jax.ShapeDtypeStruct(hist.shape, BF),
            jax.ShapeDtypeStruct(hist.shape, F32),
            jax.ShapeDtypeStruct((2, count, texts - fresh.shape[0]), BF),
            jax.ShapeDtypeStruct((2, count, texts), BF),
            jax.ShapeDtypeStruct(w_self.shape, BF),
            jax.ShapeDtypeStruct(w_neigh.shape, BF),
            jax.ShapeDtypeStruct(upstream.shape, BF),
        ),
        in_specs=scalars() + whole(1) + far_off(8),
        out_specs=tuple(whole(7)),
        scratch_shapes=[
            pltpu.SemaphoreType.DMA((9,)),
            pltpu.VMEM((count, texts), BF),
            pltpu.VMEM(sums[0].shape, BF),
            pltpu.VMEM(sums[1].shape, BF),
            pltpu.VMEM(hist.shape, BF),
            pltpu.VMEM(target.shape, jnp.int32),
            pltpu.VMEM(upstream.shape, BF),
        ],
        name="sage_head",
        **grant(48, 3000000000, 4000000),
    )(place, fresh, target, counts, *sums, hist, w_self, w_neigh, upstream)


def sage_kernel(
    fanout,
    place_ref,
    fresh_ref,
    table_ref,
    agg_ref,
    other_ref,
    texts_ref,
    w_self_ref,
    w_neigh_ref,
    upstream_ref,
    act_ref,
    weights_ref,
    terms_ref,
    send_ref,
    blocks_ref,
):
    fresh = fresh_ref[...]
    quarter = w_self_ref.shape[0]
    table = table_ref[...] + dot(other_ref[0], fresh).astype(BF)
    agg_rows = ((agg_ref[...] + dot(other_ref[1], fresh)) / fanout).astype(BF)
    pre_act = dot_nt(table, w_self_ref[...]) + dot_nt(agg_rows, w_neigh_ref[...])
    cdf = 0.5 * (1.0 + lax.erf(pre_act * math.sqrt(0.5)))
    density = jnp.exp(-0.5 * pre_act * pre_act) * (1.0 / math.sqrt(2.0 * math.pi))
    act_ref[...] = pre_act * cdf
    grad_pre = (upstream_ref[...].astype(F32).T * (cdf + pre_act * density)).astype(BF)
    chips = weights_ref.shape[0]
    for k, rows in enumerate((table, agg_rows)):
        part = slice(k * quarter, (k + 1) * quarter)
        weights_ref[:, :, part] = dot_t(rows, grad_pre).reshape(chips, -1, quarter)
        terms_ref[:, :, part] = dot_t(texts_ref[k], grad_pre).reshape(chips, -1, quarter)
    put_blocks(1 - place_ref[CORE], weights_ref, terms_ref, blocks_ref)
    send_ref[...] = blocks_ref[...].astype(BF)


def put_blocks(side, weights_ref, terms_ref, blocks_ref):
    share, own_texts = weights_ref.shape[1] // NC, terms_ref.shape[1] // NC
    for core in range(NC):

        @pl.when(side == core)
        def _():
            rows = slice(core * share, (core + 1) * share)
            blocks_ref[:, :share, :] = weights_ref[:, rows, :]
            rows = slice(core * own_texts, (core + 1) * own_texts)
            blocks_ref[:, share:, :] = terms_ref[:, rows, :]


def sage(place, fresh, table, agg, other, texts, w_self, w_neigh, upstream, fanout, chips):
    quarter, width = w_self.shape
    count = table.shape[0]
    share, own_texts = width // chips, texts.shape[2] // chips
    block = (chips, (share + own_texts) // NC, 2 * quarter)
    return pl.pallas_call(
        lambda *refs: sage_kernel(fanout, *refs),
        out_shape=(
            jax.ShapeDtypeStruct((count, quarter), F32),
            jax.ShapeDtypeStruct((chips, share, 2 * quarter), F32),
            jax.ShapeDtypeStruct((chips, own_texts, 2 * quarter), F32),
            jax.ShapeDtypeStruct(block, BF),
        ),
        in_specs=scalars() + whole(8),
        out_specs=tuple(whole(4)),
        scratch_shapes=[pltpu.VMEM(block, F32)],
        name="sage",
        **grant(16, 2000000000, 8000000),
    )(place, fresh, table, agg, other, texts, w_self, w_neigh, upstream)


def tail_kernel(place_ref, act_ref, weights_ref, terms_ref, sage_ref, keep_ref):
    sage_ref[...] = act_ref[...].T.astype(BF)
    put_blocks(place_ref[CORE], weights_ref, terms_ref, keep_ref)


def sage_tail(place, act, weights, terms, send):
    return pl.pallas_call(
        tail_kernel,
        out_shape=(
            jax.ShapeDtypeStruct(act.shape[::-1], BF),
            jax.ShapeDtypeStruct(send.shape, F32),
        ),
        in_specs=scalars() + whole(3),
        out_specs=tuple(whole(2)),
        name="sage_tail",
        **grant(16, 3000000000, 4000000),
    )(place, act, weights, terms)


def combine_kernel(keep_ref, got_ref, out_ref):
    sums = keep_ref[...] + got_ref[...].astype(F32)
    out_ref[...] = sums.astype(BF)


def combine(keep, got):
    return pl.pallas_call(
        combine_kernel,
        out_shape=jax.ShapeDtypeStruct(got.shape, BF),
        in_specs=whole(2),
        out_specs=whole(1)[0],
        name="combine",
        **grant(16, 200000, 1200000),
    )(keep, got)


def final_kernel(fanout, share, place_ref, parts_ref, w_self_ref, w_neigh_ref, *term_refs):
    quarter = w_self_ref.shape[0]
    rows = jnp.sum(parts_ref[...].astype(F32), axis=0)[share:]
    at_rows = rows[:, :quarter].astype(BF)
    at_links = (rows[:, quarter:] / fanout).astype(BF)
    terms = dot(at_rows, w_self_ref[...]) + dot(at_links, w_neigh_ref[...])
    for s, ref in enumerate(term_refs):
        ref[...] = sliced(terms, lax.rem(place_ref[ME] + s, NY), quarter)


def final_terms(place, parts, w_self, w_neigh, share, fanout):
    quarter = w_self.shape[0]
    texts = jax.ShapeDtypeStruct((parts.shape[1] - share, quarter), F32)
    return pl.pallas_call(
        lambda *refs: final_kernel(fanout, share, *refs),
        out_shape=(texts,) * NY,
        in_specs=scalars() + whole(3),
        out_specs=tuple(whole(NY)),
        name="final_terms",
        **grant(16, 10000000, 1000000),
    )(place, parts, w_self, w_neigh)


def weight_kernel(parts_ref, self_ref, neigh_ref):
    share, quarter = self_ref.shape
    total = jnp.sum(parts_ref[...].astype(F32), axis=0)
    self_ref[...] = total[:share, :quarter]
    neigh_ref[...] = total[:share, quarter:]


def final_weights(parts, share):
    grads = jax.ShapeDtypeStruct((share, parts.shape[2] // 2), F32)
    return pl.pallas_call(
        weight_kernel,
        out_shape=(grads, grads),
        in_specs=whole(1),
        out_specs=(pl.BlockSpec(),) * 2,
        name="final_weights",
        **grant(16, 3000000000, 4000000),
    )(parts)


def local(
    hidden_states,
    text_len,
    w_qkv,
    w_out,
    w_up,
    w_down,
    hist,
    nbr,
    send_rows,
    fresh_target,
    w_self,
    w_neigh,
    upstream,
):
    my_x, my_z, my_c, my_y = (lax.axis_index(axis) for axis in "xzcy")
    model_width = hist.shape[1]
    peer_count, slot_count = send_rows.shape[1:]
    fanout = nbr.shape[1]
    share = model_width // peer_count
    chips = peer_count // NC
    dom = (my_x * NZ + my_z) * NC + my_c

    texts = (NY, hidden_states.shape[0] // NY, model_width)
    context = attend(hidden_states, text_len, w_qkv)
    attended = dot(context, w_out).astype(BF).reshape(texts)

    def part(s):
        return lax.dynamic_index_in_dim(attended, (my_y + s) % NY, 0, keepdims=False)

    residual = lax.dynamic_index_in_dim(hidden_states.reshape(texts), my_y, 0, keepdims=False)
    parts = [part(0)] + [pull(part(NY - s), "y", s) for s in (2, 1, 3)]
    first_norm = first_layer_norm(residual, parts)

    target = fresh_target[None, :]
    attended, wanted, lengths = lax.optimization_barrier((attended, send_rows, text_len))
    place = jnp.concatenate([jnp.stack([dom, my_c, my_y]).astype(jnp.int32), lengths])
    wanted = wanted.reshape(peer_count * slot_count, 1)
    outgoing = outgoing_rows(place, target, wanted, hist, chips)
    received = lax.all_to_all(outgoing, ("x", "z"), split_axis=0, concat_axis=0, tiled=True)

    others = {s: pull(first_norm, "y", s) for s in (1, 3, 2)}
    own, up, down = feed_first(first_norm, w_up, w_down)
    up, late_nbr = lax.optimization_barrier((up, nbr))
    linked = link_counts(place, late_nbr.T, peer_count, slot_count)
    others[2], linked = lax.optimization_barrier((others[2], linked))
    parts = [own] + [pull(feed(others[s], up, down), "y", NY - s) for s in (1, 3, 2)]
    fresh_row = pooled_row(place, first_norm, parts)

    rows = [fresh_row] + [pull(fresh_row, "y", s) for s in (1, 3, 2)]
    _, received = lax.optimization_barrier((fresh_row, received))
    across = pull(received, "c", 1)
    sums, counts = halo_sums(place, received, across, target, linked, hist)
    rows, sums, counts = lax.optimization_barrier((rows, sums, counts))
    rows = spread_rows(rows, chips)
    fresh = lax.all_to_all(rows, ("x", "z"), split_axis=0, concat_axis=0, tiled=True)
    sums = (sums, swap(sums))
    fresh, sums = lax.optimization_barrier((fresh, sums))
    fresh = fresh.reshape(-1, model_width)
    other = pull(fresh, "c", 1)

    begun = sage_head(
        place, fresh, counts, sums, target, hist, w_self.T, w_neigh.T, upstream.T, fanout
    )
    act, weights, terms, send = sage(place, other, *begun, fanout, chips)
    sage_out, keep = sage_tail(place, act, weights, terms, send)
    parts = combine(keep, pull(send, "c", 1))
    parts = lax.all_to_all(parts, ("x", "z"), split_axis=0, concat_axis=0, tiled=True)
    grad_fresh, *terms = final_terms(place, parts, w_self.T, w_neigh.T, share, fanout)
    grad_self_w, grad_neigh_w = final_weights(parts, share)
    for s in (2, 1, 3):
        grad_fresh = grad_fresh + pull(terms[NY - s - 1], "y", s)
    return (sage_out.T, grad_fresh, grad_self_w, grad_neigh_w)


def solution(mesh):
    dom = ("x", "z", "c")
    split = Mesh(mesh.devices.reshape(NX, NZ, NC, NY), dom + ("y",))
    in_specs = (
        P(dom, None),
        P(dom),
        P(None, None, "y"),
        P("y", None),
        P(None, "y"),
        P("y", None),
        P(dom, None),
        P(dom, None),
        P(dom, None, None),
        P(),
        P(None, "y"),
        P(None, "y"),
        P(dom, "y"),
    )
    out_specs = (P(dom, "y"),) * 4
    return jax.shard_map(local, mesh=split, in_specs=in_specs, out_specs=out_specs, check_vma=False)
```
